256 devices in a mesh: expert: 32 (over y, z_hi, core), dp: 8 (over z_lo, x).
Axes of the slice: x: 4, y: 4, z: 8 (z_hi: 4, z_lo: 2; z = z_hi * 2 + z_lo), core: 2. Of those that a mesh axis runs over, the one named last changes fastest.
Arguments:
- tokens: bfloat16 [4096, 3584], P('expert', 'dp'), may hold values from -6 to 6
- expert_ids: int32 [4096, 8], P('expert'), may hold values from 0 to 31, all different within a row; in each aligned block of 128 rows (0 to 127, 128 to 255, ...) at most 40 rows name the same one
- gate_weights: float32 [4096, 8], P('expert'), may hold values from 0.05 to 0.5
- cotangent: bfloat16 [4096, 3584], P('expert', 'dp'), may hold values from -6 to 6
- holder: int32 [32], replicated, may hold values from 0 to 31, as said below
- migrations: int32 [16, 3], replicated, may hold values from 0 to 31, as said below
- inner_weight: bfloat16 [32, 3584, 2048], P('expert', 'dp'), may hold values from -0.09375 to 0.09375
- outer_weight: bfloat16 [32, 3584, 1024], P('expert', 'dp'), may hold values from -0.1875 to 0.1875
- first_moment: float32 [32, 3584, 2048], P('expert', 'dp'), may hold values from -6 to 6
- second_moment: float32 [32, 3584, 2048], P('expert', 'dp'), may hold values from 0.02 to 0.2
Outputs:
- combined: bfloat16 [4096, 3584], P('expert', 'dp')
- update_step: bfloat16 [32, 3584, 2048], P('expert', 'dp')
The draws below stay inside these ranges and needn't reach their ends.
Inputs may be any that keep to these rules, and one draw needn't show every extreme that they name: `expert_ids`: within the rows of one index of expert, no expert is named by more than 40 rows, a bound that some block reaches; each row names 8 different experts. `holder`: A permutation of the slots. `migrations`: column 0 is holder of column 1. The rows form 16 // 2 swaps: for each row (e, a, b) there is a row (holder[b], b, a); every slot is a source at most once and a == b never.
All inputs are finite; a program needn't handle non-finite values.
Results may differ from the reference program's by a relative error of at most 0.029.
Values may be sent and summed in bfloat16 or wider, within the bound.
No kernel may reach another device: no remote copies, remote signals or barrier semaphores. Data moves between devices by JAX's collectives and lax.ppermute only.
A program may use at most 128 MiB of HBM per device.

```python
import math
import jax
import jax.numpy as jnp
import numpy as np
from jax import lax

D = 3584
FF = 1024
TOPK = 8
TOK_DEV = 128
EXPERTS = 32
CAP = 40
MIGRATIONS = 16
TOKENS = 4096
N_EXPERT = 32
N_DP = 8


def shared_slots(key):
    holder = jax.random.permutation(key, EXPERTS).astype(jnp.int32)
    chosen = jax.random.permutation(jax.random.fold_in(key, 11), EXPERTS)[:MIGRATIONS].astype(jnp.int32)
    firsts = chosen[0::2]
    seconds = chosen[1::2]
    sources = jnp.concatenate([firsts, seconds])
    targets = jnp.concatenate([seconds, firsts])
    moving = holder[sources]
    return (holder, jnp.stack([moving, sources, targets], axis=1).astype(jnp.int32))


def draw_holder(key, part):
    shared = shared_slots(key)
    return shared[0]


def draw_migrations(key, part):
    shared = shared_slots(key)
    return shared[1]


def level_of(rng, dims, pieces, smallest, largest):
    gain, own = 1.0, jax.random.fold_in(rng, 6)
    for dim, blocks in pieces:
        heights = jnp.exp(jax.random.uniform(jax.random.fold_in(own, dim), (blocks,), jnp.float32, smallest / len(pieces), largest / len(pieces)))
        gain = gain * jnp.repeat(heights, dims[dim] // blocks).reshape([-1 if axis == dim else 1 for axis in range(len(dims))])
    return gain


def routed_block(own_key, own, number, rows, amount, top, limit, skew):
    sequence = jax.random.permutation(own_key, amount)
    crowded, common = load_shares(amount, rows * top, limit, skew, True), load_shares(amount, rows * top, limit, skew, False)
    places = jnp.arange(amount)

    def named(sizes, offset_by):
        used = int((sizes > 0).sum())
        fixed = max(1, used // 4)
        passed = fixed + (places - fixed + offset_by * (used - fixed)) % max(1, amount - fixed)
        return jnp.zeros((amount,), jnp.int32).at[sequence[jnp.where(places < fixed, places, passed)]].set(jnp.asarray(sizes, jnp.int32))

    sizes = jnp.where(number % 4 == 0, named(crowded, number // 4), named(common, number - number // 4 - 1))
    mixed = jax.random.permutation(jax.random.fold_in(own, 3), amount)
    donor, sink = mixed[0:amount // 2 * 2:2], mixed[1:amount // 2 * 2:2]
    room = jnp.minimum(sizes[donor] - 1, limit - sizes[sink]) // 2
    room = jnp.where((donor == sequence[0]) | (sink == sequence[0]) | (sizes[sink] == 0), 0, jnp.maximum(room, 0))
    passed = jax.random.randint(jax.random.fold_in(own, 4), (amount // 2,), 0, 1 << 20) % (room + 1)
    sizes = sizes.at[donor].add(-passed).at[sink].add(passed)
    labels = jnp.searchsorted(jnp.cumsum(sizes), jnp.arange(rows * top), side="right").astype(jnp.int32)
    listing = labels.reshape(top, rows).T
    listing = listing[jax.random.permutation(jax.random.fold_in(own, 1), rows)]
    offset_by = jax.random.randint(jax.random.fold_in(own, 2), (rows, 1), 0, top)
    return jnp.take_along_axis(listing, (jnp.arange(top)[None, :] + offset_by) % top, axis=1)


def load_shares(count, total, limit, skew, full):
    weights = [(1 << 20) // math.isqrt(standing ** skew) + 1 for standing in range(1, count + 1)]
    largest = limit if full else min(limit, max(-(-total // count), total * weights[0] // sum(weights)))
    least = 1 if total - largest >= count - 1 else 0
    holding, spare = [largest] + [least] * (count - 1), total - largest - least * (count - 1)
    while spare > 0:
        movable = [i for i in range(1, count) if holding[i] < largest] or [i for i in range(1, count) if holding[i] < limit]
        pool, remaining = sum([weights[i] for i in movable]), spare
        for i in movable:
            extra = min(limit - holding[i], max(1, remaining * weights[i] // pool), spare)
            holding[i] = holding[i] + extra
            spare = spare - extra
    return np.array(holding)


def bell_draw(stream_key, shape, scale, most, split=(), kind=jnp.bfloat16):
    values = scale * jax.random.normal(stream_key, shape, jnp.float32)
    if split:
        values = values * level_of(stream_key, shape, split, -0.22, 0.18)
    return jnp.clip(values, -most, most).astype(kind)


def setup_inputs(seed: int = 0) -> dict:
    key_of = jax.random.split(jax.random.key(seed), 11)
    tokens = bell_draw(key_of[0], (TOKENS, D), 1.0, 6.0, ((0, 32), (1, 8)))
    expert_ids_keys = jax.random.split(jax.random.fold_in(key_of[1], 1), TOKENS // TOK_DEV)
    expert_ids_turns = jax.random.permutation(jax.random.fold_in(key_of[1], 3), TOKENS // TOK_DEV)
    expert_ids = jax.vmap(lambda own, number: routed_block(jax.random.fold_in(key_of[1], 2), own, number, TOK_DEV, EXPERTS, TOPK, CAP, 1))(expert_ids_keys, expert_ids_turns).reshape((TOKENS, TOPK))
    gate_weights = jnp.clip(jnp.exp(math.log(0.5) - 2.3025851 * jax.random.uniform(key_of[2], (TOKENS, TOPK), jnp.float32) ** level_of(key_of[2], (TOKENS, TOPK), ((0, 32),), -0.2, 0.2)), 0.05, 0.5)
    cotangent = bell_draw(key_of[3], (TOKENS, D), 1.0, 6.0, ((0, 32), (1, 8)))
    holder = draw_holder(jax.random.fold_in(key_of[10], 71), 0)
    migrations = draw_migrations(jax.random.fold_in(key_of[10], 71), 0)
    inner_weight = bell_draw(key_of[6], (EXPERTS, D, 2 * FF), D ** -0.5, 0.09375, ((0, 32), (1, 8)))
    outer_weight = bell_draw(key_of[7], (EXPERTS, D, FF), FF ** -0.5, 0.1875, ((0, 32), (1, 8)))
    first_moment = bell_draw(key_of[8], (EXPERTS, D, 2 * FF), 1.0, 6.0, ((0, 32), (1, 8)), jnp.float32)
    second_moment = jnp.clip(jnp.exp(math.log(0.2) - 2.3025851 * jax.random.uniform(key_of[9], (EXPERTS, D, 2 * FF), jnp.float32) ** level_of(key_of[9], (EXPERTS, D, 2 * FF), ((0, 32), (1, 8)), -0.2, 0.2)), 0.02, 0.2)
    return dict(tokens=tokens, expert_ids=expert_ids, gate_weights=gate_weights, cotangent=cotangent, holder=holder, migrations=migrations, inner_weight=inner_weight, outer_weight=outer_weight, first_moment=first_moment, second_moment=second_moment)


beta_one = 0.9
beta_two = 0.999
epsilon = 1e-08
bias_one = 1.0 - 0.9 ** 10
bias_two = 1.0 - 0.999 ** 10

def locate(holder, migrations):
    slots = jnp.arange(EXPERTS, dtype=jnp.int32)
    home = lax.optimization_barrier(jnp.sum(jnp.where(holder[None, :] == slots[:, None], slots[None, :], 0), axis=1)).astype(jnp.int32)
    anchor = slots + lax.optimization_barrier(jnp.sum(jnp.where(migrations[None, :, 2] == slots[:, None], migrations[None, :, 1] - slots[:, None], 0), axis=1)).astype(jnp.int32)
    return (home, anchor)

def blocked_product(left, right, blocks):
    width = left.shape[1] // blocks
    total = jnp.zeros((left.shape[0], right.shape[1]), jnp.float32)
    for block in range(blocks):
        part = jnp.dot(left[:, block * width:(block + 1) * width], right[block * width:(block + 1) * width], preferred_element_type=jnp.float32)
        rounded = lax.optimization_barrier(part.astype(jnp.bfloat16))
        total = total + rounded.astype(jnp.float32)
    return total

def reference(tokens, expert_ids, gate_weights, cotangent, holder, migrations, inner_weight, outer_weight, first_moment, second_moment):
    home, anchor = locate(holder, migrations)
    capacity = N_EXPERT * CAP
    flat_ids = expert_ids.reshape(-1)
    entry_count = TOKENS * TOPK
    onehot = (flat_ids[:, None] == jnp.arange(EXPERTS, dtype=jnp.int32)[None, :]).astype(jnp.int32)
    ranks = lax.optimization_barrier(jnp.sum((jnp.cumsum(onehot, axis=0) - 1) * onehot, axis=1)).astype(jnp.int32)
    places = flat_ids * capacity + ranks
    entries = jnp.full((EXPERTS * capacity,), -1, jnp.int32).at[places].set(jnp.arange(entry_count, dtype=jnp.int32))
    entries = entries.reshape(EXPERTS, capacity)
    gate_flat = gate_weights.reshape(-1)

    def expert_work(expert):
        picked = entries[expert]
        valid = picked >= 0
        safe = jnp.where(valid, picked, 0)
        token_rows = safe // TOPK
        inputs = jnp.where(valid[:, None], tokens[token_rows], jnp.zeros((), jnp.bfloat16))
        slot = home[expert]
        inner = inner_weight[slot]
        outer = outer_weight[slot]
        pre = blocked_product(inputs, inner, N_DP)
        gate_part = pre[:, :FF]
        up_part = pre[:, FF:]
        sigma = jax.nn.sigmoid(gate_part)
        silu_value = gate_part * sigma
        hidden = (silu_value * up_part).astype(jnp.bfloat16)
        outputs = jnp.dot(hidden, outer.T, preferred_element_type=jnp.float32).astype(jnp.bfloat16)
        gate_pick = jnp.where(valid, gate_flat[safe], 0.0)
        routed = (gate_pick[:, None] * cotangent[token_rows].astype(jnp.float32)).astype(jnp.bfloat16)
        hidden_grad = blocked_product(routed, outer, N_DP)
        slope = sigma * (1.0 + gate_part * (1.0 - sigma))
        pre_grad = jnp.concatenate([hidden_grad * up_part * slope, hidden_grad * silu_value], axis=1).astype(jnp.bfloat16)
        weight_grad = jnp.dot(inputs.T, pre_grad, preferred_element_type=jnp.float32)
        new_first = beta_one * first_moment[slot] + (1.0 - beta_one) * weight_grad
        new_second = beta_two * second_moment[slot] + (1.0 - beta_two) * weight_grad * weight_grad
        step = (new_first / bias_one / (jnp.sqrt(new_second / bias_two) + epsilon)).astype(jnp.bfloat16)
        return (outputs, step)
    outputs_all, steps_all = lax.map(expert_work, jnp.arange(EXPERTS, dtype=jnp.int32))
    flat_out = outputs_all.reshape(EXPERTS * capacity, D)
    row_index = places.reshape(TOKENS, TOPK)
    combined = jnp.zeros((TOKENS, D), jnp.float32)
    for choice_index in range(TOPK):
        combined = combined + gate_weights[:, choice_index:choice_index + 1] * flat_out[row_index[:, choice_index]].astype(jnp.float32)
    update_step = steps_all[holder[anchor]]
    return (combined.astype(jnp.bfloat16), update_step)
```

```python
import functools

import jax
import jax.numpy as jnp
from jax import lax
from jax.experimental import pallas as pl
from jax.experimental.pallas import tpu as pltpu
from jax.sharding import Mesh, PartitionSpec as P

beta_one = 0.9
beta_two = 0.999
epsilon = 1e-08
bias_one = 1.0 - 0.9**10
bias_two = 1.0 - 0.999**10

bf16 = jnp.bfloat16
f32 = jnp.float32

experts = 32
capacity = 40
tok_count = 128
width = 448
hidden_units = 1024
rows = experts * capacity
group = 4
block_rows = group * capacity
order = (4, 3, 5, 6, 2, 7, 0, 1)
halves = 2
span = hidden_units // halves

expert_axes = ("y", "zh", "c")
vmem_bytes = 48 * 1024 * 1024


def shift(value, axis, by):
    n = lax.axis_size(axis)
    return lax.ppermute(value, axis, [(i, (i + by) % n) for i in range(n)])


def gather_four(value, axis):
    half = value.shape[0] // 2
    from_left = shift(value, axis, 1)
    from_right = shift(value, axis, -1)
    far_low = shift(from_left[:half], axis, 1)
    far_high = shift(from_right[half:], axis, -1)
    return value, from_right, far_low, far_high, from_left


def scatter_four(to_right, to_left, next_low, prev_high, own, axis):
    half = next_low.shape[0]
    got_left = shift(to_right, axis, 1)
    got_right = shift(to_left, axis, -1)
    second_right = (next_low.astype(f32) + got_left[:half].astype(f32)).astype(bf16)
    second_left = (prev_high.astype(f32) + got_right[:half].astype(f32)).astype(bf16)
    low = shift(second_right, axis, 1).astype(f32) + got_right[half:].astype(f32)
    high = shift(second_left, axis, -1).astype(f32) + got_left[half:].astype(f32)
    return own.astype(f32) + jnp.concatenate([low, high], axis=0)


def gather_sources(value):
    for axis in ("zh", "y"):
        own, following, far_low, far_high, previous = gather_four(value, axis)
        value = jnp.concatenate([own, following, far_low, far_high, previous], axis=0)
    return jnp.concatenate([value, shift(value, "c", 1)], axis=0)


def scatter_sources(value):
    half = value.shape[0] // 2
    value = value[:half].astype(f32) + shift(value[half:], "c", 1).astype(f32)
    for axis in ("y", "zh"):
        value = value.astype(bf16)
        n = value.shape[0] // 4
        own, following, far, previous = [value[i * n : (i + 1) * n] for i in range(4)]
        h = n // 2
        value = scatter_four(
            jnp.concatenate([far[:h], following[h:]], axis=0),
            jnp.concatenate([far[h:], previous[:h]], axis=0),
            following[:h],
            previous[h:],
            own,
            axis,
        )
    return value


def dot(a, b, contract_a=1, contract_b=0):
    return lax.dot_general(
        a, b, (((contract_a,), (contract_b,)), ((), ())), preferred_element_type=f32
    )


def placing(expert, gates):
    lane = lax.broadcasted_iota(jnp.int32, (8, 128), 1)
    row = lax.broadcasted_iota(jnp.int32, (8, 128), 0)
    pick = ((row == 0) & (lane == 64 + expert)) | ((row == 1) & (lane == 96 + expert))
    both = dot(jnp.where(pick, 1.0, 0.0).astype(bf16), gates, 1, 1)
    gate = both[0:1] + both[1:2]
    hit = jnp.where(both > 0.0, 1.0, 0.0)
    before = lax.broadcasted_iota(jnp.int32, (128, 128), 0) < lax.broadcasted_iota(
        jnp.int32, (128, 128), 1
    )
    before = jnp.where(before, 1.0, 0.0).astype(bf16)
    wanted = []
    for s in range(group):
        part = hit[:, s * 128 : (s + 1) * 128]
        rank = dot(part.astype(bf16), before) + float(capacity * s)
        wanted.append(jnp.where(part > 0.0, rank, -1.0)[0:1])
    wanted = jnp.concatenate(wanted, axis=1).astype(jnp.int32)
    at = lax.broadcasted_iota(jnp.int32, (block_rows, group * 128), 0) == wanted
    gate_rows = jnp.sum(jnp.where(at, gate, 0.0), axis=1, keepdims=True)
    return jnp.where(at, 1.0, 0.0).astype(bf16), gate_rows


def pick_rows_kernel(scaled, info, gates, values, out):
    place, gate_rows = placing(info[8], gates[...])
    picked = dot(place, values[...])[:, :width]
    if scaled:
        picked = picked * gate_rows
    out[...] = picked.astype(bf16)


def pick_rows(info, table, values, scaled):
    lanes = values.shape[1]
    return pl.pallas_call(
        functools.partial(pick_rows_kernel, scaled),
        grid_spec=pltpu.PrefetchScalarGridSpec(
            num_scalar_prefetch=1,
            grid=(8,),
            in_specs=[
                pl.BlockSpec((512, 128), lambda g, info: (info[g], 3)),
                pl.BlockSpec((512, lanes), lambda g, info: (info[g], 0)),
            ],
            out_specs=pl.BlockSpec((block_rows, width), lambda g, info: (g, 0)),
        ),
        out_shape=jax.ShapeDtypeStruct((rows, width), bf16),
        cost_estimate=pl.CostEstimate(
            flops=2 * rows * 512 * 512, bytes_accessed=6_000_000, transcendentals=0
        ),
        compiler_params=pltpu.CompilerParams(vmem_limit_bytes=vmem_bytes),
        name="pick_rows",
    )(info, table, values)


def project_kernel(left, right, to_right, to_left, next_low, prev_high, own):
    result = dot(left[...], right[...]).astype(bf16)
    to_right[...] = result[0:320]
    to_left[...] = result[320:640]
    next_low[...] = result[640:800]
    prev_high[...] = result[800:960]
    own[...] = result[960:1280]


def project(left, right, blocks, column):
    columns = 256 * blocks
    return pl.pallas_call(
        project_kernel,
        grid=(blocks,),
        in_specs=[
            pl.BlockSpec((rows, width), lambda j: (0, 0)),
            pl.BlockSpec((width, 256), lambda j: (0, column(j))),
        ],
        out_specs=[pl.BlockSpec((n, 256), lambda j: (0, j)) for n in (320, 320, 160, 160, 320)],
        out_shape=[
            jax.ShapeDtypeStruct((n, columns), bf16) for n in (320, 320, 160, 160, 320)
        ],
        cost_estimate=pl.CostEstimate(
            flops=2 * rows * width * columns,
            bytes_accessed=2 * (rows * width + width * columns + rows * columns),
            transcendentals=0,
        ),
        compiler_params=pltpu.CompilerParams(vmem_limit_bytes=vmem_bytes),
        name="project",
    )(left, right)


def sum_features(pieces):
    total = scatter_four(*pieces, "x")
    return total + shift(total.astype(bf16), "zl", 1).astype(f32)


def all_rows(value):
    own, following, far_low, far_high, previous = gather_four(value, "x")
    h = value.shape[0] // 2
    return jnp.concatenate(
        [far_low, following[h:], far_high, previous[:h], following[:h], previous[h:], own],
        axis=0,
    )


def adam_kernel(tokens, grads, first, second, step):
    weight_grad = dot(tokens[...], grads[...], 0, 0)
    new_first = beta_one * first[...] + (1.0 - beta_one) * weight_grad
    new_second = beta_two * second[...] + (1.0 - beta_two) * weight_grad * weight_grad
    result = new_first / bias_one / (jnp.sqrt(new_second / bias_two) + epsilon)
    step[0] = result[:, :128].astype(bf16)
    step[1] = result[:, 128:].astype(bf16)


def adam(tokens, grads, first, second, column):
    return pl.pallas_call(
        adam_kernel,
        grid=(4,),
        in_specs=[
            pl.BlockSpec((rows, width), lambda j: (0, 0)),
            pl.BlockSpec((rows, 256), lambda j: (0, j)),
            pl.BlockSpec((width, 256), lambda j: (0, column(j))),
            pl.BlockSpec((width, 256), lambda j: (0, column(j))),
        ],
        out_specs=pl.BlockSpec((2, width, 128), lambda j: (j, 0, 0)),
        out_shape=jax.ShapeDtypeStruct((8, width, 128), bf16),
        cost_estimate=pl.CostEstimate(
            flops=2 * rows * width * 1024,
            bytes_accessed=8_000_000,
            transcendentals=2 * width * 1024,
        ),
        compiler_params=pltpu.CompilerParams(vmem_limit_bytes=vmem_bytes),
        name="adam",
    )(tokens, grads, first, second)


def reorder_kernel(anchor, source, out):
    def one(d, carry):
        out[d] = source[anchor[d]]
        return carry

    lax.fori_loop(0, experts, one, 0)


def reorder(anchor, pieces):
    return pl.pallas_call(
        reorder_kernel,
        grid_spec=pltpu.PrefetchScalarGridSpec(
            num_scalar_prefetch=1,
            grid=(1,),
            in_specs=[pl.BlockSpec(pieces.shape, lambda g, a: (0, 0, 0))],
            out_specs=pl.BlockSpec(pieces.shape, lambda g, a: (0, 0, 0)),
        ),
        out_shape=jax.ShapeDtypeStruct(pieces.shape, bf16),
        cost_estimate=pl.CostEstimate(flops=0, bytes_accessed=2_000_000, transcendentals=0),
        compiler_params=pltpu.CompilerParams(vmem_limit_bytes=vmem_bytes),
        name="reorder",
    )(anchor, pieces)


def migrate(anchor, step):
    pieces = step.reshape(experts, width * 8 // experts, 128)
    spread = lax.all_to_all(pieces, expert_axes, split_axis=0, concat_axis=0, tiled=True)
    picked = reorder(anchor, spread)
    moved = lax.all_to_all(picked, expert_axes, split_axis=0, concat_axis=0, tiled=True)
    return moved.reshape(8, width, 128)


def place_kernel(moved, *refs):
    refs[-1][...] = moved[0]


def place(moved, base, tile):
    in_specs = [pl.BlockSpec((1, width, 128), lambda j: (j, 0, 0))]
    args = [moved]
    aliases = {}
    if base is not None:
        in_specs.append(pl.BlockSpec(memory_space=pl.ANY))
        args.append(base)
        aliases = {1: 0}
    return pl.pallas_call(
        place_kernel,
        grid=(8,),
        in_specs=in_specs,
        out_specs=pl.BlockSpec((width, 128), lambda j: (0, tile(j))),
        out_shape=jax.ShapeDtypeStruct((width, 2 * hidden_units), bf16),
        input_output_aliases=aliases,
        cost_estimate=pl.CostEstimate(flops=0, bytes_accessed=2_000_000, transcendentals=0),
        compiler_params=pltpu.CompilerParams(vmem_limit_bytes=vmem_bytes),
        name="place",
    )(*args)


def outputs_kernel(info, gates, hidden_low, hidden_high, outer, out):
    place_rows, gate_rows = placing(info[8], gates[...])
    result = dot(hidden_low[...], outer[:, :span], 1, 1)
    result = result + dot(hidden_high[...], outer[:, span:], 1, 1)
    result = (result.astype(bf16).astype(f32) * gate_rows).astype(bf16)
    out[...] = dot(place_rows, result, 0, 0).astype(bf16)


def weighted_outputs(info, table, hidden_low, hidden_high, outer):
    return pl.pallas_call(
        outputs_kernel,
        grid_spec=pltpu.PrefetchScalarGridSpec(
            num_scalar_prefetch=1,
            grid=(8,),
            in_specs=[
                pl.BlockSpec((512, 128), lambda g, info: (info[g], 3)),
                pl.BlockSpec((block_rows, span), lambda g, info: (g, 0)),
                pl.BlockSpec((block_rows, span), lambda g, info: (g, 0)),
                pl.BlockSpec((width, hidden_units), lambda g, info: (0, 0)),
            ],
            out_specs=pl.BlockSpec((512, width), lambda g, info: (info[g], 0)),
        ),
        out_shape=jax.ShapeDtypeStruct((experts * tok_count, width), bf16),
        cost_estimate=pl.CostEstimate(
            flops=2 * rows * 1536 * width, bytes_accessed=8_000_000, transcendentals=0
        ),
        compiler_params=pltpu.CompilerParams(vmem_limit_bytes=vmem_bytes),
        name="outputs",
    )(info, table, hidden_low, hidden_high, outer)


def on_device(
    tokens,
    expert_ids,
    gate_weights,
    cotangent,
    holder,
    migrations,
    inner_weight,
    outer_weight,
    first_moment,
    second_moment,
):
    slots = jnp.arange(experts, dtype=jnp.int32)
    anchor = slots + jnp.sum(
        jnp.where(
            migrations[None, :, 2] == slots[:, None], migrations[None, :, 1] - slots[:, None], 0
        ),
        axis=1,
    )
    slot = lax.axis_index(expert_axes)
    expert = jnp.sum(jnp.where(slots == slot, holder, 0))
    blocks = (2 * lax.axis_index("x") + jnp.array(order, jnp.int32)) % 8
    info = jnp.concatenate([blocks, expert[None]]).astype(jnp.int32)

    inner = inner_weight[0]
    outer = outer_weight[0]
    first = first_moment[0]
    second = second_moment[0]

    dense = jnp.zeros((tok_count, experts), f32)
    for k in range(expert_ids.shape[1]):
        dense = dense + jnp.where(
            expert_ids[:, k : k + 1] == slots[None, :], gate_weights[:, k : k + 1], 0.0
        )
    high = lax.reduce_precision(dense, 8, 7)
    table = jnp.concatenate([tokens, high.astype(bf16), (dense - high).astype(bf16)], axis=1)

    table = gather_sources(table)
    grads = gather_sources(cotangent)
    routed_tokens = pick_rows(info, table, table, False)
    routed_grads = pick_rows(info, table, grads, True)

    hidden_parts = []
    moved = None
    for h in range(halves):
        pre = sum_features(
            project(routed_tokens, inner, 4, lambda j, h=h: 2 * h + j % 2 + 4 * (j // 2))
        )
        gate_part = pre[:, :span]
        up_part = pre[:, span:]
        sigma = jax.nn.sigmoid(gate_part)
        silu_value = gate_part * sigma
        hidden_parts.append(all_rows((silu_value * up_part).astype(bf16)))
        hidden_grad = sum_features(project(routed_grads, outer, 2, lambda j, h=h: 2 * h + j))
        slope = sigma * (1.0 + gate_part * (1.0 - sigma))
        pre_grad = jnp.concatenate(
            [hidden_grad * up_part * slope, hidden_grad * silu_value], axis=1
        ).astype(bf16)
        pre_grad = all_rows(pre_grad)
        step = adam(
            routed_tokens, pre_grad, first, second, lambda j, h=h: 2 * h + j % 2 + 4 * (j // 2)
        )
        moved = place(
            migrate(anchor, step), moved, lambda j, h=h: 4 * h + j % 4 + 8 * (j // 4)
        )

    combined = scatter_sources(weighted_outputs(info, table, *hidden_parts, outer))
    return combined.astype(bf16), moved[None]


def solution(mesh):
    whole = Mesh(mesh.devices.reshape(4, 4, 2, 2, 4), ("y", "zh", "c", "zl", "x"))
    dp = ("zl", "x")
    placed = (
        P(expert_axes, dp),
        P(expert_axes, None),
        P(expert_axes, None),
        P(expert_axes, dp),
        P(),
        P(),
        P(expert_axes, dp, None),
        P(expert_axes, dp, None),
        P(expert_axes, dp, None),
        P(expert_axes, dp, None),
    )
    return jax.shard_map(
        on_device,
        mesh=whole,
        in_specs=placed,
        out_specs=(P(expert_axes, dp), P(expert_axes, dp, None)),
        check_vma=False,
    )
```

```python
import functools

import jax
import jax.numpy as jnp
from jax import lax
from jax.experimental import pallas as pl
from jax.experimental.pallas import tpu as pltpu
from jax.sharding import Mesh, PartitionSpec as P

beta_one = 0.9
beta_two = 0.999
epsilon = 1e-08
bias_one = 1.0 - 0.9**10
bias_two = 1.0 - 0.999**10

bf16 = jnp.bfloat16
f32 = jnp.float32

experts = 32
capacity = 40
tok_count = 128
width = 448
hidden_units = 1024
rows = experts * capacity
block_rows = 160
order = (4, 3, 5, 6, 2, 7, 0, 1)
chunks = ((0, 512), (512, 512))

expert_axes = ("y", "zh", "c")
vmem_bytes = 32 * 1024 * 1024


def dot(a, b, contract_a=1, contract_b=0):
    return lax.dot_general(
        a, b, (((contract_a,), (contract_b,)), ((), ())), preferred_element_type=f32
    )


def array(*shape, dtype=bf16):
    return jax.ShapeDtypeStruct(shape, dtype)


def whole(value):
    return pl.BlockSpec(value.shape, lambda *_: (0,) * len(value.shape))


class Kernels:
    def __init__(self):
        self.last = None

    def __call__(
        self,
        kernel,
        name,
        out_shape,
        inputs,
        in_specs=None,
        out_specs=None,
        grid=(1,),
        prefetch=None,
        cost=(0, 1_000_000, 0),
        aliases=None,
        order=True,
        waits=(),
        scratch=(),
    ):
        count = len(inputs) + (prefetch is not None)
        in_specs = [whole(v) for v in inputs] if in_specs is None else list(in_specs)
        if out_specs is None:
            many = isinstance(out_shape, list)
            out_specs = [whole(s) for s in out_shape] if many else whole(out_shape)
        waits = list(waits) + ([self.last] if order and self.last is not None else [])
        in_specs += [pl.BlockSpec(memory_space=pl.ANY)] * len(waits)

        def body(*refs):
            kernel(*refs[:count], *refs[count + len(waits) :])

        args = ([] if prefetch is None else [prefetch]) + list(inputs) + waits
        result = pl.pallas_call(
            body,
            out_shape=out_shape,
            grid_spec=pltpu.PrefetchScalarGridSpec(
                num_scalar_prefetch=0 if prefetch is None else 1,
                grid=grid,
                in_specs=in_specs,
                out_specs=out_specs,
                scratch_shapes=list(scratch),
            ),
            input_output_aliases=aliases or {},
            cost_estimate=pl.CostEstimate(
                flops=cost[0], bytes_accessed=cost[1], transcendentals=cost[2]
            ),
            compiler_params=pltpu.CompilerParams(vmem_limit_bytes=vmem_bytes),
            name=name,
        )(*args)
        self.last = result[-1] if isinstance(result, (list, tuple)) else result
        return result


def shift(value, axis, by):
    n = lax.axis_size(axis)
    return lax.ppermute(value, axis, [(i, (i + by) % n) for i in range(n)])


def exchange(value):
    return lax.all_to_all(value, expert_axes, split_axis=0, concat_axis=0, tiled=True)


def places_of(gates):
    hit = gates > 0.0
    before = lax.broadcasted_iota(jnp.int32, (128, 128), 0) < lax.broadcasted_iota(
        jnp.int32, (128, 128), 1
    )
    rank = dot(
        jnp.where(hit, 1.0, 0.0).astype(bf16), jnp.where(before, 1.0, 0.0).astype(bf16)
    )
    return jnp.where(hit, rank, -1.0).astype(jnp.int32)


def row_numbers():
    return lax.broadcasted_iota(jnp.int32, (capacity, tok_count), 0)


def one_hot(at):
    return jnp.where(at, 1.0, 0.0).astype(bf16)


def weights_of(at, gate):
    return jnp.sum(jnp.where(at, gate, 0.0), axis=1, keepdims=True)


def pick_kernel(gates, values, out):
    wanted = places_of(gates[...])
    at = [row_numbers() == wanted[s : s + 1] for s in range(experts)]
    place = jnp.concatenate([jnp.where(a, 1.0, 0.0) for a in at], axis=0).astype(bf16)
    out[...] = dot(place, values[...]).astype(bf16)


def gates_of_slot(slot, table, sources):
    lane = lax.broadcasted_iota(jnp.int32, (8, 128), 1)
    row = lax.broadcasted_iota(jnp.int32, (8, 128), 0)
    pick = ((row == 0) & (lane == 64 + slot)) | ((row == 1) & (lane == 96 + slot))
    both = dot(one_hot(pick), table, 1, 1)
    gate = both[0:1] + both[1:2]
    parts = [gate[:, s * 128 : (s + 1) * 128] for s in range(sources)]
    return jnp.concatenate(parts + [jnp.zeros_like(parts[0])] * (8 - sources), axis=0)


def arrive_kernel(info, table, out, gates_out, wanted_out):
    gates = gates_of_slot(info[8], table[:, 384:], 8)
    wanted = places_of(gates)
    gates_out[...] = gates
    wanted_out[...] = wanted
    picked = []
    for s in range(8):
        at = row_numbers() == wanted[s : s + 1]
        rows_of = dot(one_hot(at), table[s * 128 : (s + 1) * 128, :])[:, :width]
        picked.append(rows_of * weights_of(at, gates[s : s + 1]))
    out[...] = jnp.concatenate(picked, axis=0).astype(bf16)


def project_kernel(info, left, right, to_right, to_left, next_low, prev_high, own):
    ordered = jnp.concatenate([left[info[g]] for g in range(8)], axis=0)
    result = dot(ordered, right[...]).astype(bf16)
    to_right[...] = result[0:320]
    to_left[...] = result[320:640]
    next_low[...] = result[640:800]
    prev_high[...] = result[800:960]
    own[...] = result[960:1280]


def project(run, info, left, right, blocks, column):
    columns = 256 * blocks
    sizes = (320, 320, 160, 160, 320)
    return run(
        project_kernel,
        "project",
        [array(n, columns) for n in sizes],
        [left, right],
        in_specs=[
            pl.BlockSpec((8, block_rows, width), lambda j, info: (0, 0, 0)),
            pl.BlockSpec((width, 256), lambda j, info: (0, column(j))),
        ],
        out_specs=[pl.BlockSpec((n, 256), lambda j, info: (0, j)) for n in sizes],
        grid=(blocks,),
        prefetch=info,
        cost=(2 * rows * width * columns, 2 * rows * (width + columns), 0),
    )


def add(*values):
    total = values[0].astype(f32)
    for value in values[1:]:
        total = total + value.astype(f32)
    return total


def second_kernel(next_low, got_left, prev_high, got_right, right, left):
    right[...] = add(next_low[...], got_left[...]).astype(bf16)
    left[...] = add(prev_high[...], got_right[...]).astype(bf16)


def third_kernel(own, low, got_right, high, got_left, total):
    half = low.shape[0]
    total[:half] = add(own[:half], low[...], got_right[...]).astype(bf16)
    total[half:] = add(own[half:], high[...], got_left[...]).astype(bf16)


class RingSum:
    def __init__(self, run, pieces, axis="x"):
        self.run = run
        self.axis = axis
        to_right, to_left, self.next_low, self.prev_high, self.own = pieces
        self.columns = self.own.shape[1]
        self.block = 256 if self.columns % 256 == 0 else self.columns
        self.height = self.next_low.shape[0]
        self.got_left = shift(to_right, axis, 1)
        self.got_right = shift(to_left, axis, -1)

    def half(self, which):
        return pl.BlockSpec((self.height, self.block), lambda j: (which, j))

    def second(self):
        right, left = self.run(
            second_kernel,
            "second",
            [array(self.height, self.columns)] * 2,
            [self.next_low, self.got_left, self.prev_high, self.got_right],
            in_specs=[self.half(0)] * 4,
            out_specs=[self.half(0)] * 2,
            grid=(self.columns // self.block,),
        )
        self.low = shift(right, self.axis, 1)
        self.high = shift(left, self.axis, -1)

    def third(self, waits=()):
        both = pl.BlockSpec((2 * self.height, self.block), lambda j: (0, j))
        self.total = self.run(
            third_kernel,
            "third",
            array(2 * self.height, self.columns),
            [self.own, self.low, self.got_right, self.high, self.got_left],
            in_specs=[both, self.half(0), self.half(1), self.half(0), self.half(1)],
            out_specs=both,
            grid=(self.columns // self.block,),
            waits=waits,
        )
        return self.total

    def cross(self, waits=()):
        self.other = shift(self.third(waits), "zl", 1)

    def result(self):
        return [self.total, self.other]


def forward_kernel(from_left, from_right, low, high):
    low[...] = from_left[...]
    high[...] = from_right[...]


class RowGather:
    def __init__(self, run, value, axis="x"):
        self.run = run
        self.axis = axis
        self.own = value
        self.from_left = shift(self.own, axis, 1)
        self.from_right = shift(self.own, axis, -1)

    def second(self):
        height, columns = self.own.shape
        block = 256 if columns % 256 == 0 else columns
        first = pl.BlockSpec((height // 2, block), lambda j: (0, j))
        last = pl.BlockSpec((height // 2, block), lambda j: (1, j))
        low, high = self.run(
            forward_kernel,
            "forward",
            [array(height // 2, columns)] * 2,
            [self.from_left, self.from_right],
            in_specs=[first, last],
            out_specs=[first, first],
            grid=(columns // block,),
        )
        self.far_low = shift(low, self.axis, 1)
        self.far_high = shift(high, self.axis, -1)

    def result(self):
        return [self.own, self.from_right, self.far_low, self.far_high, self.from_left]


def hidden_kernel(*refs):
    out = refs[-1]
    at = 0
    for i in range(0, len(refs) - 1, 2):
        pre = add(refs[i][...], refs[i + 1][...])
        units = pre.shape[1] // 2
        gate, up = pre[:, :units], pre[:, units:]
        out[:, at : at + units] = (gate * jax.nn.sigmoid(gate) * up).astype(bf16)
        at += units


def hidden_of(run, sums):
    inputs = [v for s in sums for v in s.result()]
    return run(
        hidden_kernel,
        "hidden",
        array(320, hidden_units),
        inputs,
        in_specs=[pl.BlockSpec((80, v.shape[1]), lambda i: (i, 0)) for v in inputs],
        out_specs=pl.BlockSpec((80, hidden_units), lambda i: (i, 0)),
        grid=(4,),
        cost=(0, 3_000_000, 320 * hidden_units),
    )


def slope_kernel(pre, pre_other, back, back_other, out):
    p = add(pre[...], pre_other[...])
    units = p.shape[1] // 2
    gate, up = p[:, :units], p[:, units:]
    hidden_grad = add(back[...], back_other[...])
    sigma = jax.nn.sigmoid(gate)
    slope = sigma * (1.0 + gate * (1.0 - sigma))
    out[:, :units] = (hidden_grad * up * slope).astype(bf16)
    out[:, units:] = (hidden_grad * (gate * sigma)).astype(bf16)


def pre_grad_of(run, pre, back):
    inputs = pre.result() + back.result()
    columns = pre.columns
    return run(
        slope_kernel,
        "slope",
        array(320, columns),
        inputs,
        in_specs=[pl.BlockSpec((80, v.shape[1]), lambda i: (i, 0)) for v in inputs],
        out_specs=pl.BlockSpec((80, columns), lambda i: (i, 0)),
        grid=(4,),
        cost=(0, 3_000_000, 160 * columns),
    )


def ordered_rows(pieces):
    own, following, far_low, far_high, previous = [p[...] for p in pieces]
    return jnp.concatenate(
        [
            far_low,
            following[160:],
            far_high,
            previous[:160],
            following[:160],
            previous[160:],
            own,
        ],
        axis=0,
    )


def adam_kernel(info, tokens, *refs):
    pieces, (first, second, step) = refs[:5], refs[5:]
    ordered = jnp.concatenate([tokens[info[g]] for g in range(8)], axis=0)
    weight_grad = dot(ordered, ordered_rows(pieces), 0, 0)
    new_first = beta_one * first[...] + (1.0 - beta_one) * weight_grad
    new_second = beta_two * second[...] + (1.0 - beta_two) * weight_grad * weight_grad
    result = new_first / bias_one / (jnp.sqrt(new_second / bias_two) + epsilon)
    step[0] = result[:, :128].astype(bf16)
    step[1] = result[:, 128:].astype(bf16)


def adam(run, info, tokens, pieces, first, second, blocks, column):
    moments = pl.BlockSpec((width, 256), lambda j, info: (0, column(j)))
    return run(
        adam_kernel,
        "adam",
        array(2 * blocks, width, 128),
        [tokens, *pieces, first, second],
        in_specs=[pl.BlockSpec((8, block_rows, width), lambda j, info: (0, 0, 0))]
        + [pl.BlockSpec((p.shape[0], 256), lambda j, info: (0, j)) for p in pieces]
        + [moments, moments],
        out_specs=pl.BlockSpec((2, width, 128), lambda j, info: (j, 0, 0)),
        grid=(blocks,),
        prefetch=info,
        cost=(2 * rows * width * 256 * blocks, 2_000_000 * blocks, width * 512 * blocks),
    )


def reorder_kernel(anchor, source, out):
    def one(d, carry):
        out[d] = source[anchor[d]]
        return carry

    lax.fori_loop(0, experts, one, 0)


def place_kernel(moved, *refs, out):
    for i in range(moved.shape[0]):
        refs[out][:, i * 128 : (i + 1) * 128] = moved[i]


def place(run, moved, base, chunk, through=None):
    start, units = chunk
    tiles = units // 128
    anywhere = pl.BlockSpec(memory_space=pl.ANY)
    in_specs = [pl.BlockSpec((tiles, width, 128), lambda j: (j, 0, 0))]
    out_specs = [
        pl.BlockSpec(
            (width, units), lambda j: (0, start // units + j * (hidden_units // units))
        )
    ]
    inputs, shapes, aliases = [moved], [array(width, 2 * hidden_units)], {}
    for value, at in ((base, 0), (through, 1)):
        if value is None:
            continue
        aliases[len(inputs)] = at
        inputs.append(value)
        in_specs.append(anywhere)
        if at:
            shapes.append(array(*value.shape))
            out_specs.append(anywhere)
    return run(
        functools.partial(place_kernel, out=len(inputs) - 1),
        "place",
        shapes,
        inputs,
        in_specs=in_specs,
        out_specs=out_specs,
        grid=(2,),
        aliases=aliases,
    )


def outputs_kernel(info, *refs):
    pieces, (outer, gates, wanted, out_here, out_there, held) = refs[:5], refs[5:]
    g = pl.program_id(0)

    @pl.when(g == 0)
    def _():
        result = dot(ordered_rows(pieces), outer[...], 1, 1).astype(bf16).astype(f32)
        result = jnp.concatenate([result, jnp.zeros((rows, 512 - width), f32)], axis=1)
        for i in range(8):
            for s in range(4):
                at = i * block_rows + s * capacity
                held[4 * info[i] + s] = result[at : at + capacity]

    def work(first, out):
        for s in range(4):
            source = info[first + s]
            at = row_numbers() == wanted[pl.ds(source, 1), :]
            weights = weights_of(at, gates[pl.ds(source, 1), :])
            part = (held[source] * weights).astype(bf16)
            out[s * 128 : (s + 1) * 128, :] = dot(one_hot(at), part, 0, 0).astype(bf16)

    @pl.when(g < 4)
    def _():
        work(9 + 16 + 4 * g, out_there)

    @pl.when(g >= 4)
    def _():
        work(9 + 4 * (g - 4), out_here)


def split_kernel(here, other, to_right, to_left, next_low, prev_high, own):
    total = add(here[...], other[...]).astype(bf16)
    own[...] = total[0:512]
    next_low[...] = total[512:768]
    to_right[256:] = total[768:1024]
    to_right[:256] = total[1024:1280]
    to_left[:256] = total[1280:1536]
    to_left[256:] = total[1536:1792]
    prev_high[...] = total[1792:2048]


def cut_kernel(value, *outs):
    for i, out in enumerate(outs):
        out[...] = value[i * tok_count : (i + 1) * tok_count]


def sum_kernel(*refs):
    refs[-1][...] = add(*[r[...] for r in refs[:-1]])[:, :width].astype(bf16)


def on_device(
    tokens,
    expert_ids,
    gate_weights,
    cotangent,
    holder,
    migrations,
    inner_weight,
    outer_weight,
    first_moment,
    second_moment,
):
    slots = jnp.arange(experts, dtype=jnp.int32)
    anchor = slots + jnp.sum(
        jnp.where(
            migrations[None, :, 2] == slots[:, None], migrations[None, :, 1] - slots[:, None], 0
        ),
        axis=1,
    )
    slot = lax.axis_index(expert_axes)
    blocks = (2 * lax.axis_index("x") + jnp.array(order, jnp.int32)) % 8
    core, y, z = slots // 16, slots // 4 % 4, slots % 4
    relative = (
        (lax.axis_index("y") + y) % 4 * 8
        + (lax.axis_index("zh") + z) % 4 * 2
        + (lax.axis_index("c") + core) % 2
    )
    info = jnp.concatenate([blocks, slot[None], relative]).astype(jnp.int32)

    inner = inner_weight[0]
    outer = outer_weight[0]
    first = first_moment[0]
    second = second_moment[0]

    ids = expert_ids.T
    weights = gate_weights.T
    gates = jnp.zeros((experts, tok_count), f32)
    for k in range(ids.shape[0]):
        gates = gates + jnp.where(ids[k : k + 1] == holder[:, None], weights[k : k + 1], 0.0)

    high = lax.reduce_precision(gates, 8, 7)
    table = jnp.concatenate(
        [cotangent, high.T.astype(bf16), (gates - high).T.astype(bf16)], axis=1
    )
    table = lax.all_gather(table, expert_axes, axis=0, tiled=True)

    run = Kernels()
    cost = (2 * rows * 128 * 512, 2_000_000, 0)
    picked = run(pick_kernel, "pick", array(rows, width), [gates, tokens], cost=cost)
    routed_tokens = exchange(picked.reshape(experts, capacity, width))
    routed_tokens = routed_tokens.reshape(8, block_rows, width)

    def column(chunk):
        start, units = chunk
        n = units // 256
        return lambda j: start // 256 + j % n + 4 * (j // n)

    def pre_sum(chunk):
        blocks = 2 * chunk[1] // 256
        return RingSum(
            run, project(run, info, routed_tokens, inner, blocks, column(chunk))
        )

    def back_sum(chunk):
        start, units = chunk
        return RingSum(
            run,
            project(
                run, info, routed_grads, outer, units // 256, lambda j: start // 256 + j
            ),
        )

    def steps(chunk, gather):
        return adam(
            run,
            info,
            routed_tokens,
            gather.result(),
            first,
            second,
            2 * chunk[1] // 256,
            column(chunk),
        )

    def spread(step):
        return exchange(step.reshape(experts, -1, 128))

    def deliver(pieces):
        picked = run(
            reorder_kernel, "reorder", array(*pieces.shape), [pieces], prefetch=anchor
        )
        return exchange(picked).reshape(-1, width, 128)

    one, two = chunks
    pre_one = pre_sum(one)
    pre_two = pre_sum(two)
    pre_one.second()
    routed_grads, gates, wanted = run(
        arrive_kernel,
        "arrive",
        [
            array(rows, width),
            array(experts, tok_count, dtype=f32),
            array(experts, tok_count, dtype=jnp.int32),
        ],
        [table],
        in_specs=[pl.BlockSpec((1024, 512), lambda g, info: (g, 0))],
        out_specs=[
            pl.BlockSpec((2 * block_rows, width), lambda g, info: (g, 0)),
            pl.BlockSpec((8, tok_count), lambda g, info: (g, 0)),
            pl.BlockSpec((8, tok_count), lambda g, info: (g, 0)),
        ],
        grid=(4,),
        prefetch=info,
        waits=[pre_two.got_left, pre_two.got_right],
    )
    routed_grads = routed_grads.reshape(8, block_rows, width)
    back_one = back_sum(one)
    pre_one.cross()
    pre_two.second()
    back_one.second()
    back_one.cross()
    pre_two.cross()
    back_two = back_sum(two)
    grad_one = RowGather(run, pre_grad_of(run, pre_one, back_one))
    back_two.second()
    grad_one.second()
    back_two.cross()
    grad_two = RowGather(run, pre_grad_of(run, pre_two, back_two))
    hidden = RowGather(run, hidden_of(run, (pre_one, pre_two)))
    step_one = steps(one, grad_one)
    spread_one = spread(step_one)
    grad_two.second()
    hidden.second()
    moved_one = deliver(spread_one)
    step_two = steps(two, grad_two)
    update, step_two = place(run, moved_one, None, one, step_two)
    spread_two = spread(step_two)
    gathered = hidden.result()
    early = lambda g, info: (jnp.minimum(g, 3), 0)
    late = lambda g, info: (jnp.maximum(g - 4, 0), 0)
    out_here, out_there = run(
        outputs_kernel,
        "outputs",
        [array(2048, 512)] * 2,
        [*gathered, outer, gates, wanted],
        out_specs=[pl.BlockSpec((512, 512), late), pl.BlockSpec((512, 512), early)],
        grid=(8,),
        prefetch=info,
        cost=(2 * rows * hidden_units * width, 5_000_000, 0),
        scratch=[pltpu.VMEM((experts, capacity, 512), f32)],
    )
    other = shift(out_there, "c", 1)
    pieces = run(
        split_kernel,
        "split",
        [array(n, 512) for n in (512, 512, 256, 256, 512)],
        [out_here, other],
    )
    along_y = RingSum(run, pieces, "y")
    along_y.second()
    moved_two = deliver(spread_two)
    parts = run(cut_kernel, "cut", [array(tok_count, 512)] * 4, [along_y.third()])
    parts = [parts[0]] + [shift(parts[by], "zh", by) for by in (1, 2, 3)]
    combined = run(sum_kernel, "sum", array(tok_count, width), parts)
    (update,) = place(run, moved_two, update, two)
    return combined, update[None]


def solution(mesh):
    whole = Mesh(mesh.devices.reshape(4, 4, 2, 2, 4), ("y", "zh", "c", "zl", "x"))
    dp = ("zl", "x")
    placed = (
        P(expert_axes, dp),
        P(expert_axes, None),
        P(expert_axes, None),
        P(expert_axes, dp),
        P(),
        P(),
        P(expert_axes, dp, None),
        P(expert_axes, dp, None),
        P(expert_axes, dp, None),
        P(expert_axes, dp, None),
    )
    return jax.shard_map(
        on_device,
        mesh=whole,
        in_specs=placed,
        out_specs=(P(expert_axes, dp), P(expert_axes, dp, None)),
        check_vma=False,
    )
```

```python
import functools

import jax
import jax.numpy as jnp
from jax import lax
from jax.experimental import pallas as pl
from jax.experimental.pallas import tpu as pltpu
from jax.sharding import Mesh, PartitionSpec as P

beta_one = 0.9
beta_two = 0.999
epsilon = 1e-08
bias_one = 1.0 - 0.9**10
bias_two = 1.0 - 0.999**10

bf16 = jnp.bfloat16
f32 = jnp.float32

experts = 32
capacity = 40
tok_count = 128
width = 448
hidden_units = 1024
rows = experts * capacity
block_rows = 160
order = (4, 3, 5, 6, 2, 7, 0, 1)
chunks = ((0, 512), (512, 512))
span = 512

expert_axes = ("y", "zh", "c")
vmem_bytes = 32 * 1024 * 1024


def dot(a, b, contract_a=1, contract_b=0):
    return lax.dot_general(
        a, b, (((contract_a,), (contract_b,)), ((), ())), preferred_element_type=f32
    )


def array(*shape, dtype=bf16):
    return jax.ShapeDtypeStruct(shape, dtype)


def whole(value):
    return pl.BlockSpec(value.shape, lambda *_: (0,) * len(value.shape))


class Kernels:
    def __init__(self):
        self.last = None

    def __call__(
        self,
        kernel,
        name,
        out_shape,
        inputs,
        in_specs=None,
        out_specs=None,
        grid=(1,),
        prefetch=None,
        cost=(0, 1_000_000, 0),
        aliases=None,
        order=True,
        waits=(),
        scratch=(),
    ):
        count = len(inputs) + (prefetch is not None)
        in_specs = [whole(v) for v in inputs] if in_specs is None else list(in_specs)
        if out_specs is None:
            many = isinstance(out_shape, list)
            out_specs = [whole(s) for s in out_shape] if many else whole(out_shape)
        waits = list(waits) + ([self.last] if order and self.last is not None else [])
        in_specs += [pl.BlockSpec(memory_space=pl.ANY)] * len(waits)

        def body(*refs):
            kernel(*refs[:count], *refs[count + len(waits) :])

        args = ([] if prefetch is None else [prefetch]) + list(inputs) + waits
        result = pl.pallas_call(
            body,
            out_shape=out_shape,
            grid_spec=pltpu.PrefetchScalarGridSpec(
                num_scalar_prefetch=0 if prefetch is None else 1,
                grid=grid,
                in_specs=in_specs,
                out_specs=out_specs,
                scratch_shapes=list(scratch),
            ),
            input_output_aliases=aliases or {},
            cost_estimate=pl.CostEstimate(
                flops=cost[0], bytes_accessed=cost[1], transcendentals=cost[2]
            ),
            compiler_params=pltpu.CompilerParams(vmem_limit_bytes=vmem_bytes),
            name=name,
        )(*args)
        self.last = result[-1] if isinstance(result, (list, tuple)) else result
        return result


def shift(value, axis, by):
    n = lax.axis_size(axis)
    return lax.ppermute(value, axis, [(i, (i + by) % n) for i in range(n)])


def exchange(value):
    return lax.all_to_all(value, expert_axes, split_axis=0, concat_axis=0, tiled=True)


def places_of(gates):
    hit = gates > 0.0
    before = lax.broadcasted_iota(jnp.int32, (128, 128), 0) < lax.broadcasted_iota(
        jnp.int32, (128, 128), 1
    )
    rank = dot(
        jnp.where(hit, 1.0, 0.0).astype(bf16), jnp.where(before, 1.0, 0.0).astype(bf16)
    )
    return jnp.where(hit, rank, -1.0).astype(jnp.int32)


def row_numbers():
    return lax.broadcasted_iota(jnp.int32, (capacity, tok_count), 0)


def one_hot(at):
    return jnp.where(at, 1.0, 0.0).astype(bf16)


def weights_of(at, gate):
    return jnp.sum(jnp.where(at, gate, 0.0), axis=1, keepdims=True)


def pick_kernel(gates, values, out):
    wanted = places_of(gates[...])
    at = [row_numbers() == wanted[s : s + 1] for s in range(experts)]
    place = jnp.concatenate([jnp.where(a, 1.0, 0.0) for a in at], axis=0).astype(bf16)
    out[...] = dot(place, values[...]).astype(bf16)


def gates_of_slot(slot, table, sources):
    lane = lax.broadcasted_iota(jnp.int32, (8, 128), 1)
    row = lax.broadcasted_iota(jnp.int32, (8, 128), 0)
    pick = ((row == 0) & (lane == 64 + slot)) | ((row == 1) & (lane == 96 + slot))
    both = dot(one_hot(pick), table, 1, 1)
    gate = both[0:1] + both[1:2]
    parts = [gate[:, s * 128 : (s + 1) * 128] for s in range(sources)]
    return jnp.concatenate(parts + [jnp.zeros_like(parts[0])] * (8 - sources), axis=0)


def arrive_kernel(info, table, out, gates_out, wanted_out):
    gates = gates_of_slot(info[8], table[:, 384:], 8)
    wanted = places_of(gates)
    gates_out[...] = gates
    wanted_out[...] = wanted
    picked = []
    for s in range(8):
        at = row_numbers() == wanted[s : s + 1]
        rows_of = dot(one_hot(at), table[s * 128 : (s + 1) * 128, :])[:, :width]
        picked.append(rows_of * weights_of(at, gates[s : s + 1]))
    out[...] = jnp.concatenate(picked, axis=0).astype(bf16)


def project_kernel(info, left, right, to_right, to_left, next_low, prev_high, own):
    ordered = jnp.concatenate([left[info[g]] for g in range(8)], axis=0)
    result = dot(ordered, right[...]).astype(bf16)
    to_right[...] = result[0:320]
    to_left[...] = result[320:640]
    next_low[...] = result[640:800]
    prev_high[...] = result[800:960]
    own[...] = result[960:1280]


def project(run, info, left, right, blocks, column, waits=()):
    columns = 256 * blocks
    sizes = (320, 320, 160, 160, 320)
    return run(
        project_kernel,
        "project",
        [array(n, columns) for n in sizes],
        [left, right],
        in_specs=[
            pl.BlockSpec((8, block_rows, width), lambda j, info: (0, 0, 0)),
            pl.BlockSpec((width, 256), lambda j, info: (0, column(j))),
        ],
        out_specs=[pl.BlockSpec((n, 256), lambda j, info: (0, j)) for n in sizes],
        grid=(blocks,),
        prefetch=info,
        cost=(2 * rows * width * columns, 2 * rows * (width + columns), 0),
        waits=waits,
    )


def add(*values):
    total = values[0].astype(f32)
    for value in values[1:]:
        total = total + value.astype(f32)
    return total


def second_kernel(next_low, got_left, prev_high, got_right, right, left):
    right[...] = add(next_low[...], got_left[...]).astype(bf16)
    left[...] = add(prev_high[...], got_right[...]).astype(bf16)


def third_kernel(own, low, got_right, high, got_left, total):
    half = low.shape[0]
    total[:half] = add(own[:half], low[...], got_right[...]).astype(bf16)
    total[half:] = add(own[half:], high[...], got_left[...]).astype(bf16)


class RingSum:
    def __init__(self, run, pieces, axis="x"):
        self.run = run
        self.axis = axis
        to_right, to_left, self.next_low, self.prev_high, self.own = pieces
        self.columns = self.own.shape[1]
        self.block = 256 if self.columns % 256 == 0 else self.columns
        self.height = self.next_low.shape[0]
        self.got_left = shift(to_right, axis, 1)
        self.got_right = shift(to_left, axis, -1)

    def half(self, which):
        return pl.BlockSpec((self.height, self.block), lambda j: (which, j))

    def second(self, waits=()):
        right, left = self.run(
            second_kernel,
            "second",
            [array(self.height, self.columns)] * 2,
            [self.next_low, self.got_left, self.prev_high, self.got_right],
            in_specs=[self.half(0)] * 4,
            out_specs=[self.half(0)] * 2,
            grid=(self.columns // self.block,),
            waits=waits,
        )
        self.low = shift(right, self.axis, 1)
        self.high = shift(left, self.axis, -1)

    def third(self, waits=()):
        both = pl.BlockSpec((2 * self.height, self.block), lambda j: (0, j))
        self.total = self.run(
            third_kernel,
            "third",
            array(2 * self.height, self.columns),
            [self.own, self.low, self.got_right, self.high, self.got_left],
            in_specs=[both, self.half(0), self.half(1), self.half(0), self.half(1)],
            out_specs=both,
            grid=(self.columns // self.block,),
            waits=waits,
        )
        return self.total

    def cross(self, waits=()):
        self.other = shift(self.third(waits), "zl", 1)

    def result(self):
        return [self.total, self.other]


def forward_kernel(from_left, from_right, low, high):
    low[...] = from_left[...]
    high[...] = from_right[...]


class RowGather:
    def __init__(self, run, value, axis="x"):
        self.run = run
        self.axis = axis
        self.own = value
        self.from_left = shift(self.own, axis, 1)
        self.from_right = shift(self.own, axis, -1)

    def second(self):
        height, columns = self.own.shape
        block = 256 if columns % 256 == 0 else columns
        first = pl.BlockSpec((height // 2, block), lambda j: (0, j))
        last = pl.BlockSpec((height // 2, block), lambda j: (1, j))
        low, high = self.run(
            forward_kernel,
            "forward",
            [array(height // 2, columns)] * 2,
            [self.from_left, self.from_right],
            in_specs=[first, last],
            out_specs=[first, first],
            grid=(columns // block,),
        )
        self.far_low = shift(low, self.axis, 1)
        self.far_high = shift(high, self.axis, -1)

    def result(self):
        return [self.own, self.from_right, self.far_low, self.far_high, self.from_left]


def slope_kernel(pre, pre_other, back, back_other, out):
    p = add(pre[...], pre_other[...])
    units = p.shape[1] // 2
    gate, up = p[:, :units], p[:, units:]
    hidden_grad = add(back[...], back_other[...])
    sigma = jax.nn.sigmoid(gate)
    slope = sigma * (1.0 + gate * (1.0 - sigma))
    out[:, :units] = (hidden_grad * up * slope).astype(bf16)
    out[:, units : 2 * units] = (hidden_grad * (gate * sigma)).astype(bf16)


def both_kernel(pre_one, other_one, pre_two, other_two, back, back_other, out):
    slope_kernel(pre_two, other_two, back, back_other, out)
    at = pre_two.shape[1]
    for value, other in ((pre_one, other_one), (pre_two, other_two)):
        pre = add(value[...], other[...])
        units = pre.shape[1] // 2
        gate, up = pre[:, :units], pre[:, units:]
        out[:, at : at + units] = (gate * jax.nn.sigmoid(gate) * up).astype(bf16)
        at += units


def activation(run, kernel, name, sums, columns):
    inputs = [v for s in sums for v in s.result()]
    return run(
        kernel,
        name,
        array(320, columns),
        inputs,
        in_specs=[pl.BlockSpec((80, v.shape[1]), lambda i: (i, 0)) for v in inputs],
        out_specs=pl.BlockSpec((80, columns), lambda i: (i, 0)),
        grid=(4,),
    )


def ordered_rows(pieces):
    own, following, far_low, far_high, previous = [p[...] for p in pieces]
    return jnp.concatenate(
        [
            far_low,
            following[160:],
            far_high,
            previous[:160],
            following[:160],
            previous[160:],
            own,
        ],
        axis=0,
    )


def adam_kernel(info, tokens, *refs):
    pieces, (first, second, step) = refs[:5], refs[5:]
    ordered = jnp.concatenate([tokens[info[g]] for g in range(8)], axis=0)
    weight_grad = dot(ordered, ordered_rows(pieces), 0, 0)
    new_first = beta_one * first[...] + (1.0 - beta_one) * weight_grad
    new_second = beta_two * second[...] + (1.0 - beta_two) * weight_grad * weight_grad
    result = new_first / bias_one / (jnp.sqrt(new_second / bias_two) + epsilon)
    step[0] = result[:, :128].astype(bf16)
    step[1] = result[:, 128:].astype(bf16)


def adam(run, info, tokens, pieces, first, second, blocks, column):
    moments = pl.BlockSpec((width, 256), lambda j, info: (0, column(j)))
    return run(
        adam_kernel,
        "adam",
        array(2 * blocks, width, 128),
        [tokens, *pieces, first, second],
        in_specs=[pl.BlockSpec((8, block_rows, width), lambda j, info: (0, 0, 0))]
        + [pl.BlockSpec((p.shape[0], 256), lambda j, info: (0, j)) for p in pieces]
        + [moments, moments],
        out_specs=pl.BlockSpec((2, width, 128), lambda j, info: (j, 0, 0)),
        grid=(blocks,),
        prefetch=info,
        cost=(2 * rows * width * 256 * blocks, 2_000_000 * blocks, width * 512 * blocks),
    )


def merge_kernel(anchor, spread, step, out):
    height = step.shape[1]

    def one(d, carry):
        out[d, :height] = spread[anchor[d]]
        out[d, height:] = step[d]
        return carry

    lax.fori_loop(0, experts, one, 0)


def reorder_kernel(anchor, merged, out):
    height = out.shape[1]

    def one(d, carry):
        out[d] = merged[anchor[d], height:]
        return carry

    lax.fori_loop(0, experts, one, 0)


def place_kernel(first, second, out):
    for chunk, moved in enumerate((first, second)):

        @pl.when(pl.program_id(0) % 2 == chunk)
        def _():
            for piece in range(moved.shape[0]):
                at, tile = piece % 4 * 112, piece // 4 * 128
                out[at : at + 112, tile : tile + 128] = moved[piece, :112]


def place(run, first, second):
    half = experts // 2
    return run(
        place_kernel,
        "place",
        array(width, 2 * hidden_units),
        [first, second],
        in_specs=[
            pl.BlockSpec((half, *v.shape[1:]), lambda j: (j // 2, 0, 0)) for v in (first, second)
        ],
        out_specs=pl.BlockSpec((width, span), lambda j: (0, j)),
        grid=(4,),
    )


def outputs_kernel(info, *refs):
    pieces, (outer, gates, wanted, out_here, out_there, held) = refs[:5], refs[5:]
    g = pl.program_id(0)

    @pl.when(g == 0)
    def _():
        result = dot(ordered_rows(pieces), outer[...], 1, 1).astype(bf16).astype(f32)
        result = jnp.concatenate([result, jnp.zeros((rows, 512 - width), f32)], axis=1)
        for i in range(8):
            for s in range(4):
                at = i * block_rows + s * capacity
                held[4 * info[i] + s] = result[at : at + capacity]

    def work(first, out):
        for s in range(4):
            source = info[first + s]
            at = row_numbers() == wanted[pl.ds(source, 1), :]
            weights = weights_of(at, gates[pl.ds(source, 1), :])
            part = (held[source] * weights).astype(bf16)
            out[s * 128 : (s + 1) * 128, :] = dot(one_hot(at), part, 0, 0).astype(bf16)

    @pl.when(g < 4)
    def _():
        work(9 + 16 + 4 * g, out_there)

    @pl.when(g >= 4)
    def _():
        work(9 + 4 * (g - 4), out_here)


def split_kernel(here, other, to_right, to_left, next_low, prev_high, own):
    total = add(here[...], other[...]).astype(bf16)
    own[...] = total[0:512]
    next_low[...] = total[512:768]
    to_right[256:] = total[768:1024]
    to_right[:256] = total[1024:1280]
    to_left[:256] = total[1280:1536]
    to_left[256:] = total[1536:1792]
    prev_high[...] = total[1792:2048]


def cut_kernel(value, *outs):
    for i, out in enumerate(outs):
        out[...] = value[i * tok_count : (i + 1) * tok_count]


def sum_kernel(*refs):
    refs[-1][...] = add(*[r[...] for r in refs[:-1]])[:, :width].astype(bf16)


def on_device(
    tokens,
    expert_ids,
    gate_weights,
    cotangent,
    holder,
    migrations,
    inner_weight,
    outer_weight,
    first_moment,
    second_moment,
):
    slots = jnp.arange(experts, dtype=jnp.int32)
    anchor = slots + jnp.sum(
        jnp.where(
            migrations[None, :, 2] == slots[:, None], migrations[None, :, 1] - slots[:, None], 0
        ),
        axis=1,
    )
    slot = lax.axis_index(expert_axes)
    blocks = (2 * lax.axis_index("x") + jnp.array(order, jnp.int32)) % 8
    core, y, z = slots // 16, slots // 4 % 4, slots % 4
    relative = (
        (lax.axis_index("y") + y) % 4 * 8
        + (lax.axis_index("zh") + z) % 4 * 2
        + (lax.axis_index("c") + core) % 2
    )
    info = jnp.concatenate([blocks, slot[None], relative]).astype(jnp.int32)

    inner = inner_weight[0]
    outer = outer_weight[0]
    first = first_moment[0]
    second = second_moment[0]

    ids = expert_ids.T
    weights = gate_weights.T
    gates = jnp.zeros((experts, tok_count), f32)
    for k in range(ids.shape[0]):
        gates = gates + jnp.where(ids[k : k + 1] == holder[:, None], weights[k : k + 1], 0.0)

    high = lax.reduce_precision(gates, 8, 7)
    table = jnp.concatenate(
        [cotangent, high.T.astype(bf16), (gates - high).T.astype(bf16)], axis=1
    )
    table = lax.all_gather(table, expert_axes, axis=0, tiled=True)

    run = Kernels()
    cost = (2 * rows * 128 * 512, 2_000_000, 0)
    picked = run(pick_kernel, "pick", array(rows, width), [gates, tokens], cost=cost)
    routed_tokens = exchange(picked.reshape(experts, capacity, width))
    routed_tokens = routed_tokens.reshape(8, block_rows, width)

    def column(chunk):
        start, units = chunk
        n = units // 256
        return lambda j: start // 256 + j % n + 4 * (j // n)

    def pre_sum(chunk):
        blocks = 2 * chunk[1] // 256
        return RingSum(
            run, project(run, info, routed_tokens, inner, blocks, column(chunk))
        )

    def back_sum(chunk, waits=()):
        start, units = chunk
        return RingSum(
            run,
            project(
                run,
                info,
                routed_grads,
                outer,
                units // 256,
                lambda j: start // 256 + j,
                waits,
            ),
        )

    def steps(chunk, gather):
        return adam(
            run,
            info,
            routed_tokens,
            gather.result(),
            first,
            second,
            2 * chunk[1] // 256,
            column(chunk),
        )

    def spread(step):
        return exchange(step.reshape(experts, -1, 128))

    one, two = chunks
    pre_one = pre_sum(one)
    pre_two = pre_sum(two)
    pre_one.second()
    routed_grads, gates, wanted = run(
        arrive_kernel,
        "arrive",
        [
            array(rows, width),
            array(experts, tok_count, dtype=f32),
            array(experts, tok_count, dtype=jnp.int32),
        ],
        [table],
        in_specs=[pl.BlockSpec((1024, 512), lambda g, info: (g, 0))],
        out_specs=[
            pl.BlockSpec((2 * block_rows, width), lambda g, info: (g, 0)),
            pl.BlockSpec((8, tok_count), lambda g, info: (g, 0)),
            pl.BlockSpec((8, tok_count), lambda g, info: (g, 0)),
        ],
        grid=(4,),
        prefetch=info,
    )
    routed_grads = routed_grads.reshape(8, block_rows, width)
    back_one = back_sum(one, waits=[pre_two.got_left, pre_two.got_right])
    pre_one.cross()
    back_one.second()
    back_two = back_sum(two)
    back_one.cross()
    back_two.second(waits=[pre_one.other])
    pre_two.second()
    back_two.cross()
    pre_two.cross()
    grad_one = RowGather(
        run, activation(run, slope_kernel, "slope", [pre_one, back_one], pre_one.columns)
    )
    grad_one.second()
    sums = [pre_one, pre_two, back_two]
    both = RowGather(
        run,
        activation(run, both_kernel, "both", sums, pre_two.columns + hidden_units),
    )
    first_spread = spread(steps(one, grad_one))
    both.second()
    gathered = both.result()
    early = lambda g, info: (jnp.minimum(g, 3), 0)
    late = lambda g, info: (jnp.maximum(g - 4, 0), 0)
    out_here, out_there = run(
        outputs_kernel,
        "outputs",
        [array(2048, 512)] * 2,
        [*gathered, outer, gates, wanted],
        in_specs=[
            pl.BlockSpec((p.shape[0], hidden_units), lambda g, info: (0, 1)) for p in gathered
        ]
        + [whole(outer), whole(gates), whole(wanted)],
        out_specs=[pl.BlockSpec((512, 512), late), pl.BlockSpec((512, 512), early)],
        grid=(8,),
        prefetch=info,
        cost=(2 * rows * hidden_units * width, 5_000_000, 0),
        scratch=[pltpu.VMEM((experts, capacity, 512), f32)],
    )
    other = shift(out_there, "c", 1)
    step_two = steps(two, both).reshape(experts, -1, 128)
    height = step_two.shape[1]
    merged = run(
        merge_kernel,
        "merge",
        array(experts, 2 * height, 128),
        [first_spread, step_two],
        prefetch=anchor,
    )
    merged = exchange(merged)
    pieces = run(
        split_kernel,
        "split",
        [array(n, 512) for n in (512, 512, 256, 256, 512)],
        [out_here, other],
    )
    along_y = RingSum(run, pieces, "y")
    along_y.second()
    parts = run(cut_kernel, "cut", [array(tok_count, 512)] * 4, [along_y.third()])
    parts = [parts[0]] + [shift(parts[by], "zh", by) for by in (1, 2, 3)]
    combined = run(sum_kernel, "sum", array(tok_count, width), parts)
    second_spread = run(
        reorder_kernel, "reorder", array(experts, height, 128), [merged], prefetch=anchor
    )
    second_moved = exchange(second_spread)
    update = place(run, merged, second_moved)
    return combined, update[None]


def solution(mesh):
    whole = Mesh(mesh.devices.reshape(4, 4, 2, 2, 4), ("y", "zh", "c", "zl", "x"))
    dp = ("zl", "x")
    placed = (
        P(expert_axes, dp),
        P(expert_axes, None),
        P(expert_axes, None),
        P(expert_axes, dp),
        P(),
        P(),
        P(expert_axes, dp, None),
        P(expert_axes, dp, None),
        P(expert_axes, dp, None),
        P(expert_axes, dp, None),
    )
    return jax.shard_map(
        on_device,
        mesh=whole,
        in_specs=placed,
        out_specs=(P(expert_axes, dp), P(expert_axes, dp, None)),
        check_vma=False,
    )
```

```python
import functools

import jax
import jax.numpy as jnp
from jax import lax
from jax.experimental import pallas as pl
from jax.experimental.pallas import tpu as pltpu
from jax.sharding import Mesh, PartitionSpec as P

beta_one = 0.9
beta_two = 0.999
epsilon = 1e-08
bias_one = 1.0 - 0.9**10
bias_two = 1.0 - 0.999**10

bf16 = jnp.bfloat16
f32 = jnp.float32

experts = 32
capacity = 40
tok_count = 128
width = 448
hidden_units = 1024
rows = experts * capacity
block_rows = 160
order = (4, 3, 5, 6, 2, 7, 0, 1)
chunks = ((0, 512), (512, 512))
span = 512

expert_axes = ("y", "zh", "c")
vmem_bytes = 32 * 1024 * 1024


def dot(a, b, contract_a=1, contract_b=0):
    return lax.dot_general(
        a, b, (((contract_a,), (contract_b,)), ((), ())), preferred_element_type=f32
    )


def array(*shape, dtype=bf16):
    return jax.ShapeDtypeStruct(shape, dtype)


def whole(value):
    return pl.BlockSpec(value.shape, lambda *_: (0,) * len(value.shape))


class Kernels:
    def __init__(self):
        self.last = None

    def __call__(
        self,
        kernel,
        name,
        out_shape,
        inputs,
        in_specs=None,
        out_specs=None,
        grid=(1,),
        prefetch=None,
        cost=(0, 1_000_000, 0),
        aliases=None,
        order=True,
        waits=(),
        scratch=(),
    ):
        count = len(inputs) + (prefetch is not None)
        in_specs = [whole(v) for v in inputs] if in_specs is None else list(in_specs)
        if out_specs is None:
            many = isinstance(out_shape, list)
            out_specs = [whole(s) for s in out_shape] if many else whole(out_shape)
        waits = list(waits) + ([self.last] if order and self.last is not None else [])
        in_specs += [pl.BlockSpec(memory_space=pl.ANY)] * len(waits)

        def body(*refs):
            kernel(*refs[:count], *refs[count + len(waits) :])

        args = ([] if prefetch is None else [prefetch]) + list(inputs) + waits
        result = pl.pallas_call(
            body,
            out_shape=out_shape,
            grid_spec=pltpu.PrefetchScalarGridSpec(
                num_scalar_prefetch=0 if prefetch is None else 1,
                grid=grid,
                in_specs=in_specs,
                out_specs=out_specs,
                scratch_shapes=list(scratch),
            ),
            input_output_aliases=aliases or {},
            cost_estimate=pl.CostEstimate(
                flops=cost[0], bytes_accessed=cost[1], transcendentals=cost[2]
            ),
            compiler_params=pltpu.CompilerParams(vmem_limit_bytes=vmem_bytes),
            name=name,
        )(*args)
        self.last = result[-1] if isinstance(result, (list, tuple)) else result
        return result


def shift(value, axis, by):
    n = lax.axis_size(axis)
    return lax.ppermute(value, axis, [(i, (i + by) % n) for i in range(n)])


def exchange(value):
    return lax.all_to_all(value, expert_axes, split_axis=0, concat_axis=0, tiled=True)


def places_of(gates):
    hit = gates > 0.0
    before = lax.broadcasted_iota(jnp.int32, (128, 128), 0) < lax.broadcasted_iota(
        jnp.int32, (128, 128), 1
    )
    rank = dot(
        jnp.where(hit, 1.0, 0.0).astype(bf16), jnp.where(before, 1.0, 0.0).astype(bf16)
    )
    return jnp.where(hit, rank, -1.0).astype(jnp.int32)


def row_numbers():
    return lax.broadcasted_iota(jnp.int32, (capacity, tok_count), 0)


def one_hot(at):
    return jnp.where(at, 1.0, 0.0).astype(bf16)


def weights_of(at, gate):
    return jnp.sum(jnp.where(at, gate, 0.0), axis=1, keepdims=True)


def pick_kernel(gates, values, out):
    wanted = places_of(gates[...])
    at = [row_numbers() == wanted[s : s + 1] for s in range(experts)]
    place = jnp.concatenate([jnp.where(a, 1.0, 0.0) for a in at], axis=0).astype(bf16)
    out[...] = dot(place, values[...]).astype(bf16)


def gates_of_slot(slot, table, sources):
    lane = lax.broadcasted_iota(jnp.int32, (8, 128), 1)
    row = lax.broadcasted_iota(jnp.int32, (8, 128), 0)
    pick = ((row == 0) & (lane == 64 + slot)) | ((row == 1) & (lane == 96 + slot))
    both = dot(one_hot(pick), table, 1, 1)
    gate = both[0:1] + both[1:2]
    parts = [gate[:, s * 128 : (s + 1) * 128] for s in range(sources)]
    return jnp.concatenate(parts + [jnp.zeros_like(parts[0])] * (8 - sources), axis=0)


def arrive_kernel(info, table, out, gates_out, wanted_out):
    gates = gates_of_slot(info[8], table[:, 384:], 8)
    wanted = places_of(gates)
    gates_out[...] = gates
    wanted_out[...] = wanted
    picked = []
    for s in range(8):
        at = row_numbers() == wanted[s : s + 1]
        rows_of = dot(one_hot(at), table[s * 128 : (s + 1) * 128, :])[:, :width]
        picked.append(rows_of * weights_of(at, gates[s : s + 1]))
    out[...] = jnp.concatenate(picked, axis=0).astype(bf16)


def project_kernel(info, left, right, to_right, to_left, next_low, prev_high, own):
    ordered = jnp.concatenate([left[info[g]] for g in range(8)], axis=0)
    result = dot(ordered, right[...]).astype(bf16)
    to_right[...] = result[0:320]
    to_left[...] = result[320:640]
    next_low[...] = result[640:800]
    prev_high[...] = result[800:960]
    own[...] = result[960:1280]


def project(run, info, left, right, blocks, column, waits=()):
    columns = 256 * blocks
    sizes = (320, 320, 160, 160, 320)
    return run(
        project_kernel,
        "project",
        [array(n, columns) for n in sizes],
        [left, right],
        in_specs=[
            pl.BlockSpec((8, block_rows, width), lambda j, info: (0, 0, 0)),
            pl.BlockSpec((width, 256), lambda j, info: (0, column(j))),
        ],
        out_specs=[pl.BlockSpec((n, 256), lambda j, info: (0, j)) for n in sizes],
        grid=(blocks,),
        prefetch=info,
        cost=(2 * rows * width * columns, 2 * rows * (width + columns), 0),
        waits=waits,
    )


def add(*values):
    total = values[0].astype(f32)
    for value in values[1:]:
        total = total + value.astype(f32)
    return total


def second_kernel(next_low, got_left, prev_high, got_right, right, left):
    right[...] = add(next_low[...], got_left[...]).astype(bf16)
    left[...] = add(prev_high[...], got_right[...]).astype(bf16)


def third_kernel(own, low, got_right, high, got_left, total):
    half = low.shape[0]
    total[:half] = add(own[:half], low[...], got_right[...]).astype(bf16)
    total[half:] = add(own[half:], high[...], got_left[...]).astype(bf16)


class RingSum:
    def __init__(self, run, pieces, axis="x"):
        self.run = run
        self.axis = axis
        to_right, to_left, self.next_low, self.prev_high, self.own = pieces
        self.columns = self.own.shape[1]
        self.block = 256 if self.columns % 256 == 0 else self.columns
        self.height = self.next_low.shape[0]
        self.got_left = shift(to_right, axis, 1)
        self.got_right = shift(to_left, axis, -1)

    def half(self, which):
        return pl.BlockSpec((self.height, self.block), lambda j: (which, j))

    def second(self, waits=()):
        right, left = self.run(
            second_kernel,
            "second",
            [array(self.height, self.columns)] * 2,
            [self.next_low, self.got_left, self.prev_high, self.got_right],
            in_specs=[self.half(0)] * 4,
            out_specs=[self.half(0)] * 2,
            grid=(self.columns // self.block,),
            waits=waits,
        )
        self.low = shift(right, self.axis, 1)
        self.high = shift(left, self.axis, -1)

    def third(self, waits=()):
        both = pl.BlockSpec((2 * self.height, self.block), lambda j: (0, j))
        self.total = self.run(
            third_kernel,
            "third",
            array(2 * self.height, self.columns),
            [self.own, self.low, self.got_right, self.high, self.got_left],
            in_specs=[both, self.half(0), self.half(1), self.half(0), self.half(1)],
            out_specs=both,
            grid=(self.columns // self.block,),
            waits=waits,
        )
        return self.total

    def cross(self, waits=()):
        self.other = shift(self.third(waits), "zl", 1)

    def result(self):
        return [self.total, self.other]


def forward_kernel(from_left, from_right, low, high):
    low[...] = from_left[...]
    high[...] = from_right[...]


class RowGather:
    def __init__(self, run, value, axis="x"):
        self.run = run
        self.axis = axis
        self.own = value
        self.from_left = shift(self.own, axis, 1)
        self.from_right = shift(self.own, axis, -1)

    def second(self):
        height, columns = self.own.shape
        block = 1024 if columns % 1024 == 0 else columns
        first = pl.BlockSpec((height // 2, block), lambda j: (0, j))
        last = pl.BlockSpec((height // 2, block), lambda j: (1, j))
        low, high = self.run(
            forward_kernel,
            "forward",
            [array(height // 2, columns)] * 2,
            [self.from_left, self.from_right],
            in_specs=[first, last],
            out_specs=[first, first],
            grid=(columns // block,),
        )
        self.far_low = shift(low, self.axis, 1)
        self.far_high = shift(high, self.axis, -1)

    def result(self):
        return [self.own, self.from_right, self.far_low, self.far_high, self.from_left]


def slope_kernel(pre, pre_other, back, back_other, out):
    p = add(pre[...], pre_other[...])
    units = p.shape[1] // 2
    gate, up = p[:, :units], p[:, units:]
    hidden_grad = add(back[...], back_other[...])
    sigma = jax.nn.sigmoid(gate)
    slope = sigma * (1.0 + gate * (1.0 - sigma))
    out[:, :units] = (hidden_grad * up * slope).astype(bf16)
    out[:, units : 2 * units] = (hidden_grad * (gate * sigma)).astype(bf16)


def both_kernel(pre_one, other_one, pre_two, other_two, back, back_other, out):
    slope_kernel(pre_two, other_two, back, back_other, out)
    at = pre_two.shape[1]
    for value, other in ((pre_one, other_one), (pre_two, other_two)):
        pre = add(value[...], other[...])
        units = pre.shape[1] // 2
        gate, up = pre[:, :units], pre[:, units:]
        out[:, at : at + units] = (gate * jax.nn.sigmoid(gate) * up).astype(bf16)
        at += units


def activation(run, kernel, name, sums, columns):
    inputs = [v for s in sums for v in s.result()]
    return run(
        kernel,
        name,
        array(320, columns),
        inputs,
        in_specs=[pl.BlockSpec((80, v.shape[1]), lambda i: (i, 0)) for v in inputs],
        out_specs=pl.BlockSpec((80, columns), lambda i: (i, 0)),
        grid=(4,),
    )


def ordered_rows(pieces):
    own, following, far_low, far_high, previous = [p[...] for p in pieces]
    return jnp.concatenate(
        [
            far_low,
            following[160:],
            far_high,
            previous[:160],
            following[:160],
            previous[160:],
            own,
        ],
        axis=0,
    )


def adam_kernel(info, tokens, *refs):
    pieces, (first, second, step) = refs[:5], refs[5:]
    ordered = jnp.concatenate([tokens[info[g]] for g in range(8)], axis=0)
    weight_grad = dot(ordered, ordered_rows(pieces), 0, 0)
    new_first = beta_one * first[...] + (1.0 - beta_one) * weight_grad
    new_second = beta_two * second[...] + (1.0 - beta_two) * weight_grad * weight_grad
    result = new_first / bias_one / (jnp.sqrt(new_second / bias_two) + epsilon)
    step[0] = result[:, :128].astype(bf16)
    step[1] = result[:, 128:].astype(bf16)


def adam(run, info, tokens, pieces, first, second, blocks, column):
    moments = pl.BlockSpec((width, 256), lambda j, info: (0, column(j)))
    return run(
        adam_kernel,
        "adam",
        array(2 * blocks, width, 128),
        [tokens, *pieces, first, second],
        in_specs=[pl.BlockSpec((8, block_rows, width), lambda j, info: (0, 0, 0))]
        + [pl.BlockSpec((p.shape[0], 256), lambda j, info: (0, j)) for p in pieces]
        + [moments, moments],
        out_specs=pl.BlockSpec((2, width, 128), lambda j, info: (j, 0, 0)),
        grid=(blocks,),
        prefetch=info,
        cost=(2 * rows * width * 256 * blocks, 2_000_000 * blocks, width * 512 * blocks),
    )


def merge_kernel(anchor, spread, step, out):
    height = step.shape[1]

    def one(d, carry):
        out[d, :height] = spread[anchor[d]]
        out[d, height:] = step[d]
        return carry

    lax.fori_loop(0, experts, one, 0)


def reorder_kernel(anchor, merged, out):
    height = out.shape[1]

    def one(d, carry):
        out[d] = merged[anchor[d], height:]
        return carry

    lax.fori_loop(0, experts, one, 0)


def place_kernel(first, second, out):
    for chunk, moved in enumerate((first, second)):

        @pl.when(pl.program_id(0) % 2 == chunk)
        def _():
            for piece in range(moved.shape[0]):
                at, tile = piece % 4 * 112, piece // 4 * 128
                out[at : at + 112, tile : tile + 128] = moved[piece, :112]


def place(run, first, second):
    half = experts // 2
    return run(
        place_kernel,
        "place",
        array(width, 2 * hidden_units),
        [first, second],
        in_specs=[
            pl.BlockSpec((half, *v.shape[1:]), lambda j: (j // 2, 0, 0)) for v in (first, second)
        ],
        out_specs=pl.BlockSpec((width, span), lambda j: (0, j)),
        grid=(4,),
    )


def outputs_kernel(info, *refs):
    pieces, (outer, gates, wanted, out_here, out_there, held) = refs[:5], refs[5:]
    g = pl.program_id(0)

    @pl.when(g == 0)
    def _():
        result = dot(ordered_rows(pieces), outer[...], 1, 1).astype(bf16).astype(f32)
        result = jnp.concatenate([result, jnp.zeros((rows, 512 - width), f32)], axis=1)
        for i in range(8):
            for s in range(4):
                at = i * block_rows + s * capacity
                held[4 * info[i] + s] = result[at : at + capacity]

    def work(first, out):
        for s in range(4):
            source = info[first + s]
            at = row_numbers() == wanted[pl.ds(source, 1), :]
            weights = weights_of(at, gates[pl.ds(source, 1), :])
            part = (held[source] * weights).astype(bf16)
            out[s * 128 : (s + 1) * 128, :] = dot(one_hot(at), part, 0, 0).astype(bf16)

    @pl.when(g < 4)
    def _():
        work(9 + 16 + 4 * g, out_there)

    @pl.when(g >= 4)
    def _():
        work(9 + 4 * (g - 4), out_here)


def split_kernel(here, other, to_right, to_left, next_low, prev_high, own):
    total = add(here[...], other[...]).astype(bf16)
    own[...] = total[0:512]
    next_low[...] = total[512:768]
    to_right[256:] = total[768:1024]
    to_right[:256] = total[1024:1280]
    to_left[:256] = total[1280:1536]
    to_left[256:] = total[1536:1792]
    prev_high[...] = total[1792:2048]


def cut_kernel(value, *outs):
    for i, out in enumerate(outs):
        out[...] = value[i * tok_count : (i + 1) * tok_count]


def sum_kernel(*refs):
    refs[-1][...] = add(*[r[...] for r in refs[:-1]])[:, :width].astype(bf16)


def on_device(
    tokens,
    expert_ids,
    gate_weights,
    cotangent,
    holder,
    migrations,
    inner_weight,
    outer_weight,
    first_moment,
    second_moment,
):
    slots = jnp.arange(experts, dtype=jnp.int32)
    anchor = slots + jnp.sum(
        jnp.where(
            migrations[None, :, 2] == slots[:, None], migrations[None, :, 1] - slots[:, None], 0
        ),
        axis=1,
    )
    slot = lax.axis_index(expert_axes)
    blocks = (2 * lax.axis_index("x") + jnp.array(order, jnp.int32)) % 8
    core, y, z = slots // 16, slots // 4 % 4, slots % 4
    relative = (
        (lax.axis_index("y") + y) % 4 * 8
        + (lax.axis_index("zh") + z) % 4 * 2
        + (lax.axis_index("c") + core) % 2
    )
    info = jnp.concatenate([blocks, slot[None], relative]).astype(jnp.int32)

    inner = inner_weight[0]
    outer = outer_weight[0]
    first = first_moment[0]
    second = second_moment[0]

    ids = expert_ids.T
    weights = gate_weights.T
    gates = jnp.zeros((experts, tok_count), f32)
    for k in range(ids.shape[0]):
        gates = gates + jnp.where(ids[k : k + 1] == holder[:, None], weights[k : k + 1], 0.0)

    high = lax.reduce_precision(gates, 8, 7)
    table = jnp.concatenate(
        [cotangent, high.T.astype(bf16), (gates - high).T.astype(bf16)], axis=1
    )
    table = lax.all_gather(table, expert_axes, axis=0, tiled=True)

    run = Kernels()
    cost = (2 * rows * 128 * 512, 2_000_000, 0)
    picked = run(pick_kernel, "pick", array(rows, width), [gates, tokens], cost=cost)
    routed_tokens = exchange(picked.reshape(experts, capacity, width))
    routed_tokens = routed_tokens.reshape(8, block_rows, width)

    def column(chunk):
        start, units = chunk
        n = units // 256
        return lambda j: start // 256 + j % n + 4 * (j // n)

    def pre_sum(chunk):
        blocks = 2 * chunk[1] // 256
        return RingSum(
            run, project(run, info, routed_tokens, inner, blocks, column(chunk))
        )

    def back_sum(chunk, waits=()):
        start, units = chunk
        return RingSum(
            run,
            project(
                run,
                info,
                routed_grads,
                outer,
                units // 256,
                lambda j: start // 256 + j,
                waits,
            ),
        )

    def steps(chunk, gather):
        return adam(
            run,
            info,
            routed_tokens,
            gather.result(),
            first,
            second,
            2 * chunk[1] // 256,
            column(chunk),
        )

    def spread(step):
        return exchange(step.reshape(experts, -1, 128))

    one, two = chunks
    pre_one = pre_sum(one)
    pre_two = pre_sum(two)
    pre_one.second()
    routed_grads, gates, wanted = run(
        arrive_kernel,
        "arrive",
        [
            array(rows, width),
            array(experts, tok_count, dtype=f32),
            array(experts, tok_count, dtype=jnp.int32),
        ],
        [table],
        in_specs=[pl.BlockSpec((1024, 512), lambda g, info: (g, 0))],
        out_specs=[
            pl.BlockSpec((2 * block_rows, width), lambda g, info: (g, 0)),
            pl.BlockSpec((8, tok_count), lambda g, info: (g, 0)),
            pl.BlockSpec((8, tok_count), lambda g, info: (g, 0)),
        ],
        grid=(4,),
        prefetch=info,
    )
    routed_grads = routed_grads.reshape(8, block_rows, width)
    back_one = back_sum(one, waits=[pre_two.got_left, pre_two.got_right])
    pre_one.cross()
    pre_two.second()
    back_one.second()
    back_two = back_sum(two, waits=[pre_two.low, pre_two.high])
    back_one.cross(waits=[pre_one.other])
    pre_two.cross()
    back_two.second()
    grad_one = RowGather(
        run, activation(run, slope_kernel, "slope", [pre_one, back_one], pre_one.columns)
    )
    back_two.cross(waits=[pre_two.other])
    grad_one.second()
    sums = [pre_one, pre_two, back_two]
    both = RowGather(
        run,
        activation(run, both_kernel, "both", sums, pre_two.columns + hidden_units),
    )
    first_spread = spread(steps(one, grad_one))
    both.second()
    gathered = both.result()
    early = lambda g, info: (jnp.minimum(g, 3), 0)
    late = lambda g, info: (jnp.maximum(g - 4, 0), 0)
    out_here, out_there = run(
        outputs_kernel,
        "outputs",
        [array(2048, 512)] * 2,
        [*gathered, outer, gates, wanted],
        in_specs=[
            pl.BlockSpec((p.shape[0], hidden_units), lambda g, info: (0, 1)) for p in gathered
        ]
        + [whole(outer), whole(gates), whole(wanted)],
        out_specs=[pl.BlockSpec((512, 512), late), pl.BlockSpec((512, 512), early)],
        grid=(8,),
        prefetch=info,
        cost=(2 * rows * hidden_units * width, 5_000_000, 0),
        scratch=[pltpu.VMEM((experts, capacity, 512), f32)],
    )
    other = shift(out_there, "c", 1)
    step_two = steps(two, both).reshape(experts, -1, 128)
    height = step_two.shape[1]
    merged = run(
        merge_kernel,
        "merge",
        array(experts, 2 * height, 128),
        [first_spread, step_two],
        prefetch=anchor,
    )
    merged = exchange(merged)
    pieces = run(
        split_kernel,
        "split",
        [array(n, 512) for n in (512, 512, 256, 256, 512)],
        [out_here, other],
    )
    along_y = RingSum(run, pieces, "y")
    along_y.second()
    parts = run(cut_kernel, "cut", [array(tok_count, 512)] * 4, [along_y.third()])
    parts = [parts[0]] + [shift(parts[by], "zh", by) for by in (1, 2, 3)]
    combined = run(sum_kernel, "sum", array(tok_count, width), parts)
    second_spread = run(
        reorder_kernel, "reorder", array(experts, height, 128), [merged], prefetch=anchor
    )
    second_moved = exchange(second_spread)
    update = place(run, merged, second_moved)
    return combined, update[None]


def solution(mesh):
    whole = Mesh(mesh.devices.reshape(4, 4, 2, 2, 4), ("y", "zh", "c", "zl", "x"))
    dp = ("zl", "x")
    placed = (
        P(expert_axes, dp),
        P(expert_axes, None),
        P(expert_axes, None),
        P(expert_axes, dp),
        P(),
        P(),
        P(expert_axes, dp, None),
        P(expert_axes, dp, None),
        P(expert_axes, dp, None),
        P(expert_axes, dp, None),
    )
    return jax.shard_map(
        on_device,
        mesh=whole,
        in_specs=placed,
        out_specs=(P(expert_axes, dp), P(expert_axes, dp, None)),
        check_vma=False,
    )
```

```python
import functools

import jax
import jax.numpy as jnp
from jax import lax
from jax.experimental import pallas as pl
from jax.experimental.pallas import tpu as pltpu
from jax.sharding import Mesh, PartitionSpec as P

beta_one = 0.9
beta_two = 0.999
epsilon = 1e-08
bias_one = 1.0 - 0.9**10
bias_two = 1.0 - 0.999**10

bf16 = jnp.bfloat16
f32 = jnp.float32

experts = 32
capacity = 40
tok_count = 128
width = 448
hidden_units = 1024
rows = experts * capacity
block_rows = 160
order = (4, 3, 5, 6, 2, 7, 0, 1)
chunks = ((0, 512), (512, 512))
span = 512

expert_axes = ("y", "zh", "c")
vmem_bytes = 40 * 1024 * 1024


def dot(a, b, contract_a=1, contract_b=0):
    return lax.dot_general(
        a, b, (((contract_a,), (contract_b,)), ((), ())), preferred_element_type=f32
    )


def array(*shape, dtype=bf16):
    return jax.ShapeDtypeStruct(shape, dtype)


def whole(value):
    return pl.BlockSpec(value.shape, lambda *_: (0,) * len(value.shape))


class Kernels:
    def __init__(self):
        self.last = None

    def __call__(
        self,
        kernel,
        name,
        out_shape,
        inputs,
        in_specs=None,
        out_specs=None,
        grid=(1,),
        prefetch=None,
        cost=(0, 1_000_000, 0),
        aliases=None,
        order=True,
        waits=(),
        scratch=(),
    ):
        count = len(inputs) + (prefetch is not None)
        in_specs = [whole(v) for v in inputs] if in_specs is None else list(in_specs)
        if out_specs is None:
            many = isinstance(out_shape, list)
            out_specs = [whole(s) for s in out_shape] if many else whole(out_shape)
        waits = list(waits) + ([self.last] if order and self.last is not None else [])
        in_specs += [pl.BlockSpec(memory_space=pl.ANY)] * len(waits)

        def body(*refs):
            kernel(*refs[:count], *refs[count + len(waits) :])

        args = ([] if prefetch is None else [prefetch]) + list(inputs) + waits
        result = pl.pallas_call(
            body,
            out_shape=out_shape,
            grid_spec=pltpu.PrefetchScalarGridSpec(
                num_scalar_prefetch=0 if prefetch is None else 1,
                grid=grid,
                in_specs=in_specs,
                out_specs=out_specs,
                scratch_shapes=list(scratch),
            ),
            input_output_aliases=aliases or {},
            cost_estimate=pl.CostEstimate(
                flops=cost[0], bytes_accessed=cost[1], transcendentals=cost[2]
            ),
            compiler_params=pltpu.CompilerParams(vmem_limit_bytes=vmem_bytes),
            name=name,
        )(*args)
        self.last = result[-1] if isinstance(result, (list, tuple)) else result
        return result


def shift(value, axis, by):
    n = lax.axis_size(axis)
    return lax.ppermute(value, axis, [(i, (i + by) % n) for i in range(n)])


def exchange(value):
    return lax.all_to_all(value, expert_axes, split_axis=0, concat_axis=0, tiled=True)


def places_of(gates):
    hit = gates > 0.0
    before = lax.broadcasted_iota(jnp.int32, (128, 128), 0) < lax.broadcasted_iota(
        jnp.int32, (128, 128), 1
    )
    rank = dot(
        jnp.where(hit, 1.0, 0.0).astype(bf16), jnp.where(before, 1.0, 0.0).astype(bf16)
    )
    return jnp.where(hit, rank, -1.0).astype(jnp.int32)


def row_numbers():
    return lax.broadcasted_iota(jnp.int32, (capacity, tok_count), 0)


def one_hot(at):
    return jnp.where(at, 1.0, 0.0).astype(bf16)


def weights_of(at, gate):
    return jnp.sum(jnp.where(at, gate, 0.0), axis=1, keepdims=True)


def pick_kernel(gates, values, out):
    wanted = places_of(gates[...])
    at = [row_numbers() == wanted[s : s + 1] for s in range(experts)]
    place = jnp.concatenate([jnp.where(a, 1.0, 0.0) for a in at], axis=0).astype(bf16)
    out[...] = dot(place, values[...]).astype(bf16)


def gates_of_slot(slot, table, sources):
    lane = lax.broadcasted_iota(jnp.int32, (8, 128), 1)
    row = lax.broadcasted_iota(jnp.int32, (8, 128), 0)
    pick = ((row == 0) & (lane == 64 + slot)) | ((row == 1) & (lane == 96 + slot))
    both = dot(one_hot(pick), table, 1, 1)
    gate = both[0:1] + both[1:2]
    parts = [gate[:, s * 128 : (s + 1) * 128] for s in range(sources)]
    return jnp.concatenate(parts + [jnp.zeros_like(parts[0])] * (8 - sources), axis=0)


def arrive_kernel(info, table, out, gates_out, wanted_out):
    gates = gates_of_slot(info[8], table[:, 384:], 8)
    wanted = places_of(gates)
    gates_out[...] = gates
    wanted_out[...] = wanted
    picked = []
    for s in range(8):
        at = row_numbers() == wanted[s : s + 1]
        rows_of = dot(one_hot(at), table[s * 128 : (s + 1) * 128, :])[:, :width]
        picked.append(rows_of * weights_of(at, gates[s : s + 1]))
    out[...] = jnp.concatenate(picked, axis=0).astype(bf16)


def project_kernel(info, left, right, to_right, to_left, next_low, prev_high, own):
    ordered = jnp.concatenate([left[info[g]] for g in range(8)], axis=0)
    result = dot(ordered, right[...]).astype(bf16)
    to_right[...] = result[0:320]
    to_left[...] = result[320:640]
    next_low[...] = result[640:800]
    prev_high[...] = result[800:960]
    own[...] = result[960:1280]


def project(run, info, left, right, blocks, column, waits=()):
    columns = 256 * blocks
    sizes = (320, 320, 160, 160, 320)
    return run(
        project_kernel,
        "project",
        [array(n, columns) for n in sizes],
        [left, right],
        in_specs=[
            pl.BlockSpec((8, block_rows, width), lambda j, info: (0, 0, 0)),
            pl.BlockSpec((width, 256), lambda j, info: (0, column(j))),
        ],
        out_specs=[pl.BlockSpec((n, 256), lambda j, info: (0, j)) for n in sizes],
        grid=(blocks,),
        prefetch=info,
        cost=(2 * rows * width * columns, 2 * rows * (width + columns), 0),
        waits=waits,
    )


def add(*values):
    total = values[0].astype(f32)
    for value in values[1:]:
        total = total + value.astype(f32)
    return total


def second_kernel(next_low, got_left, prev_high, got_right, right, left):
    right[...] = add(next_low[...], got_left[...]).astype(bf16)
    left[...] = add(prev_high[...], got_right[...]).astype(bf16)


def third_kernel(own, low, got_right, high, got_left, total):
    half = low.shape[0]
    total[:half] = add(own[:half], low[...], got_right[...]).astype(bf16)
    total[half:] = add(own[half:], high[...], got_left[...]).astype(bf16)


class RingSum:
    def __init__(self, run, pieces, axis="x"):
        self.run = run
        self.axis = axis
        to_right, to_left, self.next_low, self.prev_high, self.own = pieces
        self.columns = self.own.shape[1]
        self.block = 256 if self.columns % 256 == 0 else self.columns
        self.height = self.next_low.shape[0]
        self.got_left = shift(to_right, axis, 1)
        self.got_right = shift(to_left, axis, -1)

    def half(self, which):
        return pl.BlockSpec((self.height, self.block), lambda j: (which, j))

    def second(self, waits=()):
        right, left = self.run(
            second_kernel,
            "second",
            [array(self.height, self.columns)] * 2,
            [self.next_low, self.got_left, self.prev_high, self.got_right],
            in_specs=[self.half(0)] * 4,
            out_specs=[self.half(0)] * 2,
            grid=(self.columns // self.block,),
            waits=waits,
        )
        self.low = shift(right, self.axis, 1)
        self.high = shift(left, self.axis, -1)

    def third(self, waits=()):
        both = pl.BlockSpec((2 * self.height, self.block), lambda j: (0, j))
        self.total = self.run(
            third_kernel,
            "third",
            array(2 * self.height, self.columns),
            [self.own, self.low, self.got_right, self.high, self.got_left],
            in_specs=[both, self.half(0), self.half(1), self.half(0), self.half(1)],
            out_specs=both,
            grid=(self.columns // self.block,),
            waits=waits,
        )
        return self.total

    def cross(self, waits=()):
        self.other = shift(self.third(waits), "zl", 1)

    def result(self):
        return [self.total, self.other]


def forward_kernel(from_left, from_right, low, high):
    low[...] = from_left[...]
    high[...] = from_right[...]


class RowGather:
    def __init__(self, run, value, axis="x"):
        self.run = run
        self.axis = axis
        self.own = value
        self.from_left = shift(self.own, axis, 1)
        self.from_right = shift(self.own, axis, -1)

    def second(self):
        height, columns = self.own.shape
        block = 1024 if columns % 1024 == 0 else columns
        first = pl.BlockSpec((height // 2, block), lambda j: (0, j))
        last = pl.BlockSpec((height // 2, block), lambda j: (1, j))
        low, high = self.run(
            forward_kernel,
            "forward",
            [array(height // 2, columns)] * 2,
            [self.from_left, self.from_right],
            in_specs=[first, last],
            out_specs=[first, first],
            grid=(columns // block,),
        )
        self.far_low = shift(low, self.axis, 1)
        self.far_high = shift(high, self.axis, -1)

    def result(self):
        return [self.own, self.from_right, self.far_low, self.far_high, self.from_left]


def slope_kernel(pre, pre_other, back, back_other, out):
    p = add(pre[...], pre_other[...])
    units = p.shape[1] // 2
    gate, up = p[:, :units], p[:, units:]
    hidden_grad = add(back[...], back_other[...])
    sigma = jax.nn.sigmoid(gate)
    slope = sigma * (1.0 + gate * (1.0 - sigma))
    out[:, :units] = (hidden_grad * up * slope).astype(bf16)
    out[:, units : 2 * units] = (hidden_grad * (gate * sigma)).astype(bf16)


def both_kernel(pre_one, other_one, pre_two, other_two, back, back_other, out):
    slope_kernel(pre_two, other_two, back, back_other, out)
    at = pre_two.shape[1]
    for value, other in ((pre_one, other_one), (pre_two, other_two)):
        pre = add(value[...], other[...])
        units = pre.shape[1] // 2
        gate, up = pre[:, :units], pre[:, units:]
        out[:, at : at + units] = (gate * jax.nn.sigmoid(gate) * up).astype(bf16)
        at += units


def activation(run, kernel, name, sums, columns):
    inputs = [v for s in sums for v in s.result()]
    return run(
        kernel,
        name,
        array(320, columns),
        inputs,
        in_specs=[pl.BlockSpec((80, v.shape[1]), lambda i: (i, 0)) for v in inputs],
        out_specs=pl.BlockSpec((80, columns), lambda i: (i, 0)),
        grid=(4,),
    )


def ordered_rows(pieces):
    own, following, far_low, far_high, previous = [p[...] for p in pieces]
    return jnp.concatenate(
        [
            far_low,
            following[160:],
            far_high,
            previous[:160],
            following[:160],
            previous[160:],
            own,
        ],
        axis=0,
    )


def adam_kernel(info, tokens, *refs):
    pieces, (first, second, step) = refs[:5], refs[5:]
    ordered = jnp.concatenate([tokens[info[g]] for g in range(8)], axis=0)
    weight_grad = dot(ordered, ordered_rows(pieces), 0, 0)
    new_first = beta_one * first[...] + (1.0 - beta_one) * weight_grad
    new_second = beta_two * second[...] + (1.0 - beta_two) * weight_grad * weight_grad
    result = new_first / bias_one / (jnp.sqrt(new_second / bias_two) + epsilon)
    step[0] = result[:, :128].astype(bf16)
    step[1] = result[:, 128:].astype(bf16)


def adam(run, info, tokens, pieces, first, second, blocks, column):
    moments = pl.BlockSpec((width, 256), lambda j, info: (0, column(j)))
    return run(
        adam_kernel,
        "adam",
        array(2 * blocks, width, 128),
        [tokens, *pieces, first, second],
        in_specs=[pl.BlockSpec((8, block_rows, width), lambda j, info: (0, 0, 0))]
        + [pl.BlockSpec((p.shape[0], 256), lambda j, info: (0, j)) for p in pieces]
        + [moments, moments],
        out_specs=pl.BlockSpec((2, width, 128), lambda j, info: (j, 0, 0)),
        grid=(blocks,),
        prefetch=info,
        cost=(2 * rows * width * 256 * blocks, 2_000_000 * blocks, width * 512 * blocks),
    )


def merge_kernel(anchor, spread, step, out):
    height = step.shape[1]

    def one(d, carry):
        out[d, :height] = spread[anchor[d]]
        out[d, height:] = step[d]
        return carry

    lax.fori_loop(0, experts, one, 0)


def reorder_kernel(anchor, merged, out):
    height = out.shape[1]

    def one(d, carry):
        out[d] = merged[anchor[d], height:]
        return carry

    lax.fori_loop(0, experts, one, 0)


def place_kernel(first, second, out):
    for chunk, moved in enumerate((first, second)):

        @pl.when(pl.program_id(0) % 2 == chunk)
        def _():
            for piece in range(moved.shape[0]):
                at, tile = piece % 4 * 112, piece // 4 * 128
                out[at : at + 112, tile : tile + 128] = moved[piece, :112]


def place(run, first, second):
    half = experts // 2
    return run(
        place_kernel,
        "place",
        array(width, 2 * hidden_units),
        [first, second],
        in_specs=[
            pl.BlockSpec((half, *v.shape[1:]), lambda j: (j // 2, 0, 0)) for v in (first, second)
        ],
        out_specs=pl.BlockSpec((width, span), lambda j: (0, j)),
        grid=(4,),
    )


def outputs_kernel(info, *refs):
    pieces, (outer, gates, wanted, out_here, out_there, held) = refs[:5], refs[5:]
    g = pl.program_id(0)

    @pl.when(g == 0)
    def _():
        result = dot(ordered_rows(pieces), outer[...], 1, 1).astype(bf16).astype(f32)
        result = jnp.concatenate([result, jnp.zeros((rows, 512 - width), f32)], axis=1)
        for i in range(8):
            for s in range(4):
                at = i * block_rows + s * capacity
                held[4 * info[i] + s] = result[at : at + capacity]

    def work(first, out):
        for s in range(4):
            source = info[first + s]
            at = row_numbers() == wanted[pl.ds(source, 1), :]
            weights = weights_of(at, gates[pl.ds(source, 1), :])
            part = (held[source] * weights).astype(bf16)
            out[s * 128 : (s + 1) * 128, :] = dot(one_hot(at), part, 0, 0).astype(bf16)

    @pl.when(g < 4)
    def _():
        work(9 + 16 + 4 * g, out_there)

    @pl.when(g >= 4)
    def _():
        work(9 + 4 * (g - 4), out_here)


def split_kernel(here, other, to_right, to_left, next_low, prev_high, own):
    total = add(here[...], other[...]).astype(bf16)
    own[...] = total[0:512]
    next_low[...] = total[512:768]
    to_right[256:] = total[768:1024]
    to_right[:256] = total[1024:1280]
    to_left[:256] = total[1280:1536]
    to_left[256:] = total[1536:1792]
    prev_high[...] = total[1792:2048]


def cut_kernel(value, *outs):
    for i, out in enumerate(outs):
        out[...] = value[i * tok_count : (i + 1) * tok_count]


def sum_kernel(*refs):
    refs[-1][...] = add(*[r[...] for r in refs[:-1]])[:, :width].astype(bf16)


def on_device(
    tokens,
    expert_ids,
    gate_weights,
    cotangent,
    holder,
    migrations,
    inner_weight,
    outer_weight,
    first_moment,
    second_moment,
):
    slots = jnp.arange(experts, dtype=jnp.int32)
    anchor = slots + jnp.sum(
        jnp.where(
            migrations[None, :, 2] == slots[:, None], migrations[None, :, 1] - slots[:, None], 0
        ),
        axis=1,
    )
    slot = lax.axis_index(expert_axes)
    blocks = (2 * lax.axis_index("x") + jnp.array(order, jnp.int32)) % 8
    core, y, z = slots // 16, slots // 4 % 4, slots % 4
    relative = (
        (lax.axis_index("y") + y) % 4 * 8
        + (lax.axis_index("zh") + z) % 4 * 2
        + (lax.axis_index("c") + core) % 2
    )
    info = jnp.concatenate([blocks, slot[None], relative]).astype(jnp.int32)

    inner = inner_weight[0]
    outer = outer_weight[0]
    first = first_moment[0]
    second = second_moment[0]

    ids = expert_ids.T
    weights = gate_weights.T
    gates = jnp.zeros((experts, tok_count), f32)
    for k in range(ids.shape[0]):
        gates = gates + jnp.where(ids[k : k + 1] == holder[:, None], weights[k : k + 1], 0.0)

    high = lax.reduce_precision(gates, 8, 7)
    table = jnp.concatenate(
        [cotangent, high.T.astype(bf16), (gates - high).T.astype(bf16)], axis=1
    )
    table = lax.all_gather(table, expert_axes, axis=0, tiled=True)

    run = Kernels()
    cost = (2 * rows * 128 * 512, 2_000_000, 0)
    picked = run(pick_kernel, "pick", array(rows, width), [gates, tokens], cost=cost)
    routed_tokens = exchange(picked.reshape(experts, capacity, width))
    routed_tokens = routed_tokens.reshape(8, block_rows, width)

    def column(chunk):
        start, units = chunk
        n = units // 256
        return lambda j: start // 256 + j % n + 4 * (j // n)

    def pre_sum(chunk):
        blocks = 2 * chunk[1] // 256
        return RingSum(
            run, project(run, info, routed_tokens, inner, blocks, column(chunk))
        )

    def back_sum(chunk, waits=()):
        start, units = chunk
        return RingSum(
            run,
            project(
                run,
                info,
                routed_grads,
                outer,
                units // 256,
                lambda j: start // 256 + j,
                waits,
            ),
        )

    def steps(chunk, gather):
        return adam(
            run,
            info,
            routed_tokens,
            gather.result(),
            first,
            second,
            2 * chunk[1] // 256,
            column(chunk),
        )

    def spread(step):
        return exchange(step.reshape(experts, -1, 128))

    one, two = chunks
    pre_one = pre_sum(one)
    pre_two = pre_sum(two)
    pre_one.second()
    routed_grads, gates, wanted = run(
        arrive_kernel,
        "arrive",
        [
            array(rows, width),
            array(experts, tok_count, dtype=f32),
            array(experts, tok_count, dtype=jnp.int32),
        ],
        [table],
        in_specs=[pl.BlockSpec((1024, 512), lambda g, info: (g, 0))],
        out_specs=[
            pl.BlockSpec((2 * block_rows, width), lambda g, info: (g, 0)),
            pl.BlockSpec((8, tok_count), lambda g, info: (g, 0)),
            pl.BlockSpec((8, tok_count), lambda g, info: (g, 0)),
        ],
        grid=(4,),
        prefetch=info,
    )
    routed_grads = routed_grads.reshape(8, block_rows, width)
    back_one = back_sum(one, waits=[pre_two.got_left, pre_two.got_right])
    pre_one.cross()
    pre_two.second()
    back_one.second()
    back_two = back_sum(two, waits=[pre_two.low, pre_two.high])
    back_one.cross(waits=[pre_one.other])
    pre_two.cross()
    back_two.second()
    grad_one = RowGather(
        run, activation(run, slope_kernel, "slope", [pre_one, back_one], pre_one.columns)
    )
    back_two.cross(waits=[pre_two.other])
    grad_one.second()
    sums = [pre_one, pre_two, back_two]
    both = RowGather(
        run,
        activation(run, both_kernel, "both", sums, pre_two.columns + hidden_units),
    )
    first_spread = spread(steps(one, grad_one))
    both.second()
    step_two = steps(two, both).reshape(experts, -1, 128)
    height = step_two.shape[1]
    merged = run(
        merge_kernel,
        "merge",
        array(experts, 2 * height, 128),
        [first_spread, step_two],
        prefetch=anchor,
    )
    merged = exchange(merged)
    gathered = both.result()
    early = lambda g, info: (jnp.minimum(g, 3), 0)
    late = lambda g, info: (jnp.maximum(g - 4, 0), 0)
    out_here, out_there = run(
        outputs_kernel,
        "outputs",
        [array(2048, 512)] * 2,
        [*gathered, outer, gates, wanted],
        in_specs=[
            pl.BlockSpec((p.shape[0], hidden_units), lambda g, info: (0, 1)) for p in gathered
        ]
        + [whole(outer), whole(gates), whole(wanted)],
        out_specs=[pl.BlockSpec((512, 512), late), pl.BlockSpec((512, 512), early)],
        grid=(8,),
        prefetch=info,
        cost=(2 * rows * hidden_units * width, 5_000_000, 0),
        scratch=[pltpu.VMEM((experts, capacity, 512), f32)],
    )
    other = shift(out_there, "c", 1)
    pieces = run(
        split_kernel,
        "split",
        [array(n, 512) for n in (512, 512, 256, 256, 512)],
        [out_here, other],
    )
    along_y = RingSum(run, pieces, "y")
    along_y.second()
    by_rows = along_y.third()
    second_spread = run(
        reorder_kernel, "reorder", array(experts, height, 128), [merged], prefetch=anchor
    )
    second_moved = exchange(second_spread)
    parts = run(cut_kernel, "cut", [array(tok_count, 512)] * 4, [by_rows])
    parts = [parts[0]] + [shift(parts[by], "zh", by) for by in (1, 2, 3)]
    combined = run(sum_kernel, "sum", array(tok_count, width), parts)
    update = place(run, merged, second_moved)
    return combined, update[None]


def solution(mesh):
    whole = Mesh(mesh.devices.reshape(4, 4, 2, 2, 4), ("y", "zh", "c", "zl", "x"))
    dp = ("zl", "x")
    placed = (
        P(expert_axes, dp),
        P(expert_axes, None),
        P(expert_axes, None),
        P(expert_axes, dp),
        P(),
        P(),
        P(expert_axes, dp, None),
        P(expert_axes, dp, None),
        P(expert_axes, dp, None),
        P(expert_axes, dp, None),
    )
    return jax.shard_map(
        on_device,
        mesh=whole,
        in_specs=placed,
        out_specs=(P(expert_axes, dp), P(expert_axes, dp, None)),
        check_vma=False,
    )
```
